32 devices in a mesh: own: 8 (over y, x, core), qry: 4 (over z).
Axes of the slice: x: 2, y: 2, z: 4, core: 2. Of those that a mesh axis runs over, the one named last changes fastest.
Arguments:
- queries: bfloat16 [4, 64, 8192], P('qry', 'own'), may hold values from -6 to 6
- block_ids: int32 [4, 64], P('qry', 'own'), may hold values from 0 to 1
- left_factor: bfloat16 [2, 64, 64], P(None, 'qry'), may hold values from -0.75 to 0.75
- right_factor: bfloat16 [2, 128, 128], P(None, 'qry'), may hold values from -0.5 to 0.5
- clip_grads: bfloat16 [4096, 8192], P('own'), may hold values from -6 to 6
- lengths: int32 [4096], P('own'), may hold values from 1 to 64
Outputs:
- scores: float32 [4, 64, 4096], P('qry', 'own')
The draws below stay inside these ranges and needn't reach their ends.
All inputs are finite; a program needn't handle non-finite values.
Results may differ from the reference program's by a relative error of at most 0.0029.
Values may be sent and summed in bfloat16 or wider, within the bound.
No kernel may reach another device: no remote copies, remote signals or barrier semaphores. Data moves between devices by JAX's collectives and lax.ppermute only.
A program may use at most 64 MiB of HBM per device.

```python
import jax
import jax.numpy as jnp
from jax import lax

FA = 64
FB = 128
W = 8192
BLOCKS = 2
SETS = 4
SETROWS = 64
CLIPS = 4096


def place_ends(values, own_key, smallest, high):
    shape = values.shape
    index_at = [jax.random.randint(jax.random.fold_in(own_key, axis), (), 0, shape[axis]) for axis in range(len(shape))]
    values = values.at[tuple(index_at)].set(smallest)
    longest = shape.index(max(shape))
    index_at[longest] = (index_at[longest] + 1) % shape[longest]
    return values.at[tuple(index_at)].set(high)


def block_scale(stream_key, extent, cuts, low, largest):
    def one(position, blocks):
        steps = jax.random.uniform(jax.random.fold_in(jax.random.fold_in(stream_key, 6), position), (blocks,), jnp.float32, low / len(cuts), largest / len(cuts))
        return jnp.repeat(jnp.exp(steps), extent[position] // blocks).reshape((-1,) + (1,) * (len(extent) - position - 1))

    loudness = one(*cuts[0])
    for cut in cuts[1:]:
        loudness = loudness * one(*cut)
    return loudness


def gaussian(key, extent, spread, bound, pieces=(), dtype=jnp.bfloat16):
    values = spread * jax.random.normal(key, extent, jnp.float32)
    if pieces:
        values = values * block_scale(key, extent, pieces, -0.22, 0.18)
    return jnp.clip(values, -bound, bound).astype(dtype)


def setup_inputs(seed: int = 0) -> dict:
    seeds = jax.random.split(jax.random.key(seed), 7)
    queries = gaussian(seeds[0], (SETS, SETROWS, W), 1.0, 6.0, ((0, 4), (1, 8)))
    block_ids = place_ends(jax.random.randint(seeds[1], (SETS, SETROWS), 0, BLOCKS), jax.random.fold_in(seeds[1], 1), 0, BLOCKS - 1).astype(jnp.int32)
    left_factor = gaussian(seeds[2], (BLOCKS, FA, FA), FA ** -0.5, 0.75, ((1, 4),))
    right_factor = gaussian(seeds[3], (BLOCKS, FB, FB), FB ** -0.5, 0.5, ((1, 4),))
    clip_grads = gaussian(seeds[4], (CLIPS, W), 1.0, 6.0, ((0, 8),))
    lengths = place_ends(jax.random.randint(seeds[5], (CLIPS,), 1, 65), jax.random.fold_in(seeds[5], 1), 1, 64).astype(jnp.int32)
    return dict(queries=queries, block_ids=block_ids, left_factor=left_factor, right_factor=right_factor, clip_grads=clip_grads, lengths=lengths)


def reference(queries, block_ids, left_factor, right_factor, clip_grads, lengths):
    flat_ids = block_ids.reshape(-1)
    left_rows = left_factor.astype(jnp.float32)[flat_ids]
    right_rows = right_factor.astype(jnp.float32)[flat_ids]
    matrix = queries.reshape(-1, FA, FB).astype(jnp.float32)
    inner = jnp.einsum('nac,ncd->nad', left_rows, matrix, precision=lax.Precision.HIGHEST)
    outer = jnp.einsum('nad,nde->nae', inner, right_rows, precision=lax.Precision.HIGHEST)
    preconditioned = outer.reshape(-1, FA * FB).astype(jnp.bfloat16)
    raw = jnp.dot(preconditioned, clip_grads.T, preferred_element_type=jnp.float32)
    factor = lax.rsqrt(jnp.float32(FA * FB) * lengths.astype(jnp.float32))
    scores = raw * factor[None, :]
    return scores.reshape(queries.shape[0], queries.shape[1], -1)
```

```python
import jax
import jax.numpy as jnp
from jax import lax
from jax.experimental import pallas as pl
from jax.experimental.pallas import tpu as pltpu
from jax.sharding import PartitionSpec as P

LANES = 128
CORES = 2
VMEM = pl.BlockSpec(memory_space=pltpu.VMEM)
HBM = pl.BlockSpec(memory_space=pltpu.HBM)
F32 = jnp.float32
BF16 = jnp.bfloat16


def precondition(rows, id_values, left_full, right_full):
    blocks = left_full.shape[0]
    order_a = left_full.shape[1]
    order_b = right_full.shape[1]
    labels = jnp.arange(blocks)
    onehot = (id_values[:, :, None] == labels[None, None, :]).astype(F32)
    left_rows = jnp.einsum("srk,kac->srac", onehot, left_full.astype(F32), precision=lax.Precision.HIGHEST)
    right_rows = jnp.einsum("srk,kde->srde", onehot, right_full.astype(F32), precision=lax.Precision.HIGHEST)
    matrix = rows.reshape(rows.shape[0], rows.shape[1], order_a, order_b).astype(F32)
    inner = jnp.einsum("srac,srcd->srad", left_rows, matrix, precision=lax.Precision.HIGHEST)
    outer = jnp.einsum("srad,srde->srae", inner, right_rows, precision=lax.Precision.HIGHEST)
    return outer.reshape(rows.shape).astype(BF16)


def per_device_gathered(queries, block_ids, left_factor, right_factor, clip_grads, lengths):
    left_full = lax.all_gather(left_factor, "qry", axis=1, tiled=True)
    right_full = lax.all_gather(right_factor, "qry", axis=1, tiled=True)
    prepared = precondition(queries, block_ids, left_full, right_full)
    tiles = jnp.einsum(
        "srw,cw->src",
        lax.all_gather(prepared, "own", axis=1, tiled=True),
        clip_grads,
        preferred_element_type=F32,
    )
    factor = lax.rsqrt(F32(queries.shape[2]) * lengths.astype(F32))
    return lax.all_to_all(tiles * factor[None, None, :], "own", split_axis=1, concat_axis=2, tiled=True)


def pack_kernel(q_hbm, ids_ref, left_ref, right_ref, row_ref, fac_ref, sem):
    width = q_hbm.shape[1]
    cut = left_ref.shape[1]
    copy = pltpu.make_async_copy(q_hbm, row_ref.at[:, :width], sem)
    copy.start()
    row_ref[:, width:] = jnp.broadcast_to(ids_ref[...].astype(F32), (row_ref.shape[0], LANES)).astype(BF16)
    fac_ref[0, :, :cut, : left_ref.shape[2]] = left_ref[...]
    fac_ref[0, :, :cut, left_ref.shape[2] :] = jnp.zeros(
        (left_ref.shape[0], cut, LANES - left_ref.shape[2]), BF16
    )
    fac_ref[0, :, cut:, :] = right_ref[...]
    copy.wait()


def pack(queries, block_ids, left, right):
    rows, width = queries.shape
    blocks, cut = left.shape[:2]
    depth = cut + right.shape[1]
    return pl.pallas_call(
        pack_kernel,
        out_shape=(
            jax.ShapeDtypeStruct((rows, width + LANES), BF16),
            jax.ShapeDtypeStruct((1, blocks, depth, LANES), BF16),
        ),
        in_specs=[HBM, VMEM, VMEM, VMEM],
        out_specs=(VMEM, VMEM),
        scratch_shapes=[pltpu.SemaphoreType.DMA(())],
        compiler_params=pltpu.CompilerParams(vmem_limit_bytes=8 << 20),
    )(queries, block_ids.reshape(rows, 1), left, right)


def score_kernel(order_a, order_b, steps, *refs):
    nslots = 8
    slots = refs[:nslots]
    fac_refs = refs[nslots : nslots + steps + 1]
    clips_ref, len_ref, mine_ref, other_ref, left_s, right_s, in_s, out_s, prep_s = refs[nslots + steps + 1 :]
    rows = slots[0].shape[0]
    blocks = fac_refs[0].shape[1]
    planes = 2**steps
    cut_a, cut_b = order_a // planes, order_b // planes
    plane = lax.axis_index("qry")
    for m in range(planes):
        step = m.bit_length()
        piece = fac_refs[step][m - (1 << (step - 1)) if step else 0]
        at = lax.bitwise_xor(plane, m)
        for k in range(blocks):
            left_s[pl.ds(pl.multiple_of(k * order_a + at * cut_a, 16), cut_a), :] = piece[k, :cut_a, :order_a]
            for half in range(2):
                right_s[
                    pl.ds(pl.multiple_of(half * order_b + at * cut_b, 16), cut_b),
                    k * order_b : (k + 1) * order_b,
                ] = piece[k, cut_a:, :]
    left_all = left_s[...]
    right_all = right_s[...]
    width = order_a * order_b
    pair = 2 * rows
    for group in range(nslots // 2):
        for half in range(2):
            ref = slots[2 * group + half]
            for a in range(order_a):
                in_s[a * pair + half * rows : a * pair + half * rows + rows, :] = ref[
                    :, a * order_b : (a + 1) * order_b
                ].astype(F32)
        for n in range(0, pair, 2):
            ref = slots[2 * group + n // rows]
            x = jnp.concatenate(
                [in_s[pl.ds(n + j, order_a, stride=pair), :].astype(BF16) for j in range(2)], axis=1
            )
            inner = jnp.dot(left_all, x, preferred_element_type=F32)
            split = []
            ids = []
            for j in range(2):
                label = ref[(n + j) % rows : (n + j) % rows + 1, width:].astype(F32)
                ids.append(label)
                one = inner[:order_a, j * order_b : (j + 1) * order_b]
                for k in range(1, blocks):
                    one = jnp.where(
                        label > k - 0.5,
                        inner[k * order_a : (k + 1) * order_a, j * order_b : (j + 1) * order_b],
                        one,
                    )
                high = one.astype(BF16)
                low = (one - high.astype(F32)).astype(BF16)
                split.append(jnp.concatenate([high, low], axis=1))
            outer = jnp.dot(jnp.concatenate(split, axis=0), right_all, preferred_element_type=F32)
            for j in range(2):
                one = outer[j * order_a : (j + 1) * order_a, :order_b]
                for k in range(1, blocks):
                    one = jnp.where(
                        ids[j] > k - 0.5,
                        outer[j * order_a : (j + 1) * order_a, k * order_b : (k + 1) * order_b],
                        one,
                    )
                out_s[pl.ds(n + j, order_a, stride=pair), :] = one
        for a in range(order_a):
            prep_s[group * pair : (group + 1) * pair, a * order_b : (a + 1) * order_b] = out_s[
                a * pair : (a + 1) * pair, :
            ].astype(BF16)
    raw = lax.dot_general(
        clips_ref[...], prep_s[...], (((1,), (1,)), ((), ())), preferred_element_type=F32
    )
    factor = lax.rsqrt(F32(width) * len_ref[...].astype(F32))
    scores = raw.T * factor
    for m in range(nslots // 2):
        mine_ref[m] = scores[m * rows : (m + 1) * rows]
        other_ref[m] = scores[(m + nslots // 2) * rows : (m + nslots // 2 + 1) * rows]


def score(slots, factors, clip_grads, lengths, order_a, order_b):
    rows = slots[0].shape[0]
    clips, width = clip_grads.shape
    blocks = factors[0].shape[1]
    steps = len(factors) - 1
    half = len(slots) // 2
    kernel = lambda *refs: score_kernel(order_a, order_b, steps, *refs)
    return pl.pallas_call(
        kernel,
        out_shape=(jax.ShapeDtypeStruct((half, rows, clips), F32),) * 2,
        in_specs=[VMEM] * (len(slots) + len(factors) + 2),
        out_specs=(VMEM, VMEM),
        scratch_shapes=[
            pltpu.VMEM((blocks * order_a, order_a), BF16),
            pltpu.VMEM((2 * order_b, blocks * order_b), BF16),
            pltpu.VMEM((order_a * 2 * rows, order_b), F32),
            pltpu.VMEM((order_a * 2 * rows, order_b), F32),
            pltpu.VMEM((len(slots) * rows, width), BF16),
        ],
        compiler_params=pltpu.CompilerParams(vmem_limit_bytes=24 << 20),
        cost_estimate=pl.CostEstimate(
            flops=2 * len(slots) * rows * width * (clips + 1000), bytes_accessed=clips * width * 2, transcendentals=0
        ),
    )(*slots, *factors, clip_grads, lengths.reshape(1, clips))


def place_kernel(mine_ref, got_ref, a_ref, b_ref, d_ref, out_ref, sems):
    clips = mine_ref.shape[2]
    index = lax.axis_index("own")
    core = lax.rem(index, CORES)
    chip = lax.div(index, CORES)
    copies = []

    def put(source, chip_of, core_of, sem):
        at = pl.multiple_of((chip_of * CORES + core_of) * clips, clips)
        copy = pltpu.make_async_copy(source, out_ref.at[:, pl.ds(at, clips)], sem)
        copy.start()
        copies.append(copy)

    put(mine_ref.at[0], chip, core, sems.at[0])
    put(got_ref.at[0], chip, 1 - core, sems.at[1])
    for j, (ref, flip) in enumerate(((a_ref, 1 + core), (b_ref, 2 - core), (d_ref, 3))):
        there = lax.bitwise_xor(chip, flip)
        put(ref.at[0], there, core, sems.at[2 + 2 * j])
        put(ref.at[1], there, 1 - core, sems.at[3 + 2 * j])
    for copy in copies:
        copy.wait()


def place(mine, got, a, b, d):
    _, rows, clips = mine.shape
    return pl.pallas_call(
        place_kernel,
        out_shape=jax.ShapeDtypeStruct((rows, 8 * clips), F32),
        in_specs=[VMEM] * 5,
        out_specs=HBM,
        scratch_shapes=[pltpu.SemaphoreType.DMA((8,))],
        compiler_params=pltpu.CompilerParams(vmem_limit_bytes=8 << 20),
    )(mine, got, a, b, d)


def per_device_exchanged(planes, queries, block_ids, left_factor, right_factor, clip_grads, lengths):
    size = 4 * CORES

    def move(x, to):
        return lax.ppermute(x, "own", [(i, to(i // CORES, i % CORES)) for i in range(size)])

    def sibling(x):
        return move(x, lambda chip, core: chip * CORES + 1 - core)

    def across(x, flips):
        return move(x, lambda chip, core: (chip ^ flips[core]) * CORES + core)

    flips_a, flips_b, flips_d = (1, 2), (2, 1), (3, 3)
    row, fac = pack(queries[0], block_ids[0], left_factor, right_factor)
    slot_d = across(row, flips_d)
    slot_a = across(row, flips_a)
    slot_b = across(row, flips_b)
    factors = [fac]
    held = fac
    step = 1
    while step < planes:
        got = lax.ppermute(held, "qry", [(i, i ^ step) for i in range(planes)])
        factors.append(got)
        if step * 2 < planes:
            held = jnp.concatenate([held, got])
        step *= 2
    own = [row, slot_a, slot_b, slot_d]
    slots = own + [sibling(x) for x in own]
    order_a, order_b = left_factor.shape[2], right_factor.shape[2]
    mine, other = score(slots, factors, clip_grads, lengths, order_a, order_b)
    got = sibling(other)
    back = [
        across(jnp.stack([mine[j], got[j]]), flips) for j, flips in ((1, flips_a), (2, flips_b), (3, flips_d))
    ]
    return place(mine, got, *back)[None]


def solution(mesh):
    owners, planes = mesh.shape["own"], mesh.shape["qry"]

    def per_device(queries, block_ids, left_factor, right_factor, clip_grads, lengths):
        whole_tiles = left_factor.shape[1] % 16 == 0 and right_factor.shape[1] % 16 == 0
        if owners == 4 * CORES and planes & (planes - 1) == 0 and whole_tiles:
            return per_device_exchanged(
                planes, queries, block_ids, left_factor, right_factor, clip_grads, lengths
            )
        return per_device_gathered(queries, block_ids, left_factor, right_factor, clip_grads, lengths)

    in_specs = (
        P("qry", "own", None),
        P("qry", "own"),
        P(None, "qry", None),
        P(None, "qry", None),
        P("own", None),
        P("own"),
    )
    out_specs = P("qry", "own", None)
    return jax.shard_map(
        per_device, mesh=mesh, in_specs=in_specs, out_specs=out_specs, check_vma=False
    )
```

```python
import jax
import jax.numpy as jnp
from jax import lax
from jax.experimental import pallas as pl
from jax.experimental.pallas import tpu as pltpu
from jax.sharding import PartitionSpec as P

LANES = 128
CORES = 2
HEAD = 256
SOME_VMEM = 16 << 20
VMEM = pl.BlockSpec(memory_space=pltpu.VMEM)
HBM = pl.BlockSpec(memory_space=pltpu.HBM)
F32 = jnp.float32
BF16 = jnp.bfloat16


def precondition(rows, id_values, left_full, right_full):
    blocks = left_full.shape[0]
    order_a = left_full.shape[1]
    order_b = right_full.shape[1]
    labels = jnp.arange(blocks)
    onehot = (id_values[:, :, None] == labels[None, None, :]).astype(F32)
    left_rows = jnp.einsum("srk,kac->srac", onehot, left_full.astype(F32), precision=lax.Precision.HIGHEST)
    right_rows = jnp.einsum("srk,kde->srde", onehot, right_full.astype(F32), precision=lax.Precision.HIGHEST)
    matrix = rows.reshape(rows.shape[0], rows.shape[1], order_a, order_b).astype(F32)
    inner = jnp.einsum("srac,srcd->srad", left_rows, matrix, precision=lax.Precision.HIGHEST)
    outer = jnp.einsum("srad,srde->srae", inner, right_rows, precision=lax.Precision.HIGHEST)
    return outer.reshape(rows.shape).astype(BF16)


def per_device_gathered(queries, block_ids, left_factor, right_factor, clip_grads, lengths):
    left_full = lax.all_gather(left_factor, "qry", axis=1, tiled=True)
    right_full = lax.all_gather(right_factor, "qry", axis=1, tiled=True)
    prepared = precondition(queries, block_ids, left_full, right_full)
    tiles = jnp.einsum(
        "srw,cw->src",
        lax.all_gather(prepared, "own", axis=1, tiled=True),
        clip_grads,
        preferred_element_type=F32,
    )
    factor = lax.rsqrt(F32(queries.shape[2]) * lengths.astype(F32))
    return lax.all_to_all(tiles * factor[None, None, :], "own", split_axis=1, concat_axis=2, tiled=True)


def pack_kernel(q_hbm, ids_hbm, left_hbm, right_hbm, row_ref, fac_ref, ids_s, left_s, right_s, sems):
    rows, width = q_hbm.shape
    blocks, cut, order_a = left_s.shape
    copies = [
        pltpu.make_async_copy(left_hbm, left_s, sems.at[0]),
        pltpu.make_async_copy(right_hbm, right_s, sems.at[1]),
        pltpu.make_async_copy(ids_hbm, ids_s, sems.at[2]),
        pltpu.make_async_copy(q_hbm, row_ref.at[:, :width], sems.at[3]),
    ]
    for copy in copies:
        copy.start()
    copies[2].wait()
    square = (rows, rows)
    diagonal = lax.broadcasted_iota(jnp.int32, square, 0) == lax.broadcasted_iota(jnp.int32, square, 1)
    labels = jnp.where(diagonal, jnp.broadcast_to(ids_s[...].astype(F32), square), 0.0)
    column = jnp.sum(labels, axis=1, keepdims=True)
    row_ref[:, width:] = jnp.broadcast_to(column, (rows, LANES)).astype(BF16)
    copies[0].wait()
    copies[1].wait()
    fac_ref[0, :, :cut, :order_a] = left_s[...]
    fac_ref[0, :, :cut, order_a:] = jnp.zeros((blocks, cut, LANES - order_a), BF16)
    fac_ref[0, :, cut:, :] = right_s[...]
    copies[3].wait()


def pack(queries, block_ids, left, right):
    rows, width = queries.shape
    blocks, cut = left.shape[:2]
    depth = cut + right.shape[1]
    return pl.pallas_call(
        pack_kernel,
        out_shape=(
            jax.ShapeDtypeStruct((rows, width + LANES), BF16),
            jax.ShapeDtypeStruct((1, blocks, depth, LANES), BF16),
        ),
        in_specs=[HBM] * 4,
        out_specs=(VMEM, VMEM),
        scratch_shapes=[
            pltpu.VMEM(block_ids.shape, block_ids.dtype),
            pltpu.VMEM(left.shape, left.dtype),
            pltpu.VMEM(right.shape, right.dtype),
            pltpu.SemaphoreType.DMA((4,)),
        ],
        compiler_params=pltpu.CompilerParams(vmem_limit_bytes=SOME_VMEM),
    )(*(pltpu.with_memory_space_constraint(x, pltpu.HBM) for x in (queries, block_ids, left, right)))


def factor_kernel(order_a, order_b, steps, *refs):
    fac_refs = refs[: steps + 1]
    left_ref, right_ref = refs[steps + 1 :]
    blocks = fac_refs[0].shape[1]
    planes = 2**steps
    cut_a, cut_b = order_a // planes, order_b // planes
    plane = lax.axis_index("qry")
    for m in range(planes):
        step = m.bit_length()
        piece = fac_refs[step][m - (1 << (step - 1)) if step else 0]
        at = lax.bitwise_xor(plane, m)
        for k in range(blocks):
            left_ref[pl.ds(pl.multiple_of(k * order_a + at * cut_a, 16), cut_a), :] = piece[k, :cut_a, :order_a]
            for half in range(2):
                right_ref[
                    pl.ds(pl.multiple_of(half * order_b + at * cut_b, 16), cut_b),
                    k * order_b : (k + 1) * order_b,
                ] = piece[k, cut_a:, :]


def place_factors(factors, order_a, order_b):
    blocks = factors[0].shape[1]
    return pl.pallas_call(
        lambda *refs: factor_kernel(order_a, order_b, len(factors) - 1, *refs),
        out_shape=(
            jax.ShapeDtypeStruct((blocks * order_a, order_a), BF16),
            jax.ShapeDtypeStruct((2 * order_b, blocks * order_b), BF16),
        ),
        in_specs=[VMEM] * len(factors),
        out_specs=(VMEM, VMEM),
        compiler_params=pltpu.CompilerParams(vmem_limit_bytes=8 << 20),
        cost_estimate=pl.CostEstimate(flops=10**10, bytes_accessed=10**6, transcendentals=0),
    )(*factors)


def score_kernel(order_a, order_b, *refs):
    nslots = 8
    slots = refs[:nslots]
    (left_ref, right_ref, first_ref, len_ref, mine_ref, other_ref, in_s, out_s, prep_s) = refs[
        nslots:
    ]
    rows = slots[0].shape[0]
    blocks = left_ref.shape[0] // order_a
    left_all = left_ref[...]
    right_all = right_ref[...]
    width = order_a * order_b
    pair = 2 * rows
    for group in range(nslots // 2):
        for half in range(2):
            ref = slots[2 * group + half]
            for a in range(order_a):
                in_s[a * pair + half * rows : a * pair + half * rows + rows, :] = ref[
                    :, a * order_b : (a + 1) * order_b
                ].astype(F32)
        for n in range(0, pair, 2):
            ref = slots[2 * group + n // rows]
            x = jnp.concatenate(
                [in_s[pl.ds(n + j, order_a, stride=pair), :].astype(BF16) for j in range(2)], axis=1
            )
            inner = jnp.dot(left_all, x, preferred_element_type=F32)
            split = []
            ids = []
            for j in range(2):
                label = ref[(n + j) % rows : (n + j) % rows + 1, width:].astype(F32)
                ids.append(label)
                one = inner[:order_a, j * order_b : (j + 1) * order_b]
                for k in range(1, blocks):
                    one = jnp.where(
                        label > k - 0.5,
                        inner[k * order_a : (k + 1) * order_a, j * order_b : (j + 1) * order_b],
                        one,
                    )
                high = one.astype(BF16)
                low = (one - high.astype(F32)).astype(BF16)
                split.append(jnp.concatenate([high, low], axis=1))
            outer = jnp.dot(jnp.concatenate(split, axis=0), right_all, preferred_element_type=F32)
            for j in range(2):
                one = outer[j * order_a : (j + 1) * order_a, :order_b]
                for k in range(1, blocks):
                    one = jnp.where(
                        ids[j] > k - 0.5,
                        outer[j * order_a : (j + 1) * order_a, k * order_b : (k + 1) * order_b],
                        one,
                    )
                out_s[pl.ds(n + j, order_a, stride=pair), :] = one
        for a in range(order_a):
            prep_s[group * pair : (group + 1) * pair, a * order_b : (a + 1) * order_b] = out_s[
                a * pair : (a + 1) * pair, :
            ].astype(BF16)
    def multiply(clips_ref, start):
        count = clips_ref.shape[0]
        raw = lax.dot_general(
            clips_ref[...], prep_s[...], (((1,), (1,)), ((), ())), preferred_element_type=F32
        )
        factor = lax.rsqrt(F32(width) * len_ref[:, start : start + count].astype(F32))
        scores = raw.T * factor
        for m in range(nslots // 2):
            mine_ref[m, :, start : start + count] = scores[m * rows : (m + 1) * rows]
            other_ref[m, :, start : start + count] = scores[(m + nslots // 2) * rows : (m + nslots // 2 + 1) * rows]

    multiply(first_ref, 0)


def in_hbm(x):
    return pltpu.with_memory_space_constraint(x, pltpu.HBM)


def score(slots, left_all, right_all, clip_grads, lengths, order_a, order_b):
    rows = slots[0].shape[0]
    clips, width = clip_grads.shape
    half = len(slots) // 2
    return pl.pallas_call(
        lambda *refs: score_kernel(order_a, order_b, *refs),
        out_shape=(jax.ShapeDtypeStruct((half, rows, clips), F32),) * 2,
        in_specs=[VMEM] * (len(slots) + 4),
        out_specs=(VMEM, VMEM),
        scratch_shapes=[
            pltpu.VMEM((order_a * 2 * rows, order_b), F32),
            pltpu.VMEM((order_a * 2 * rows, order_b), F32),
            pltpu.VMEM((len(slots) * rows, width), BF16),
        ],
        compiler_params=pltpu.CompilerParams(vmem_limit_bytes=SOME_VMEM),
        cost_estimate=pl.CostEstimate(
            flops=2 * len(slots) * rows * width * (clips + 1000), bytes_accessed=clips * width * 2, transcendentals=0
        ),
    )(*slots, left_all, right_all, clip_grads, lengths.reshape(1, clips))


def place_kernel(mine_ref, got_ref, d_ref, a_ref, b_ref, out_ref, sems):
    clips = mine_ref.shape[2]
    index = lax.axis_index("own")
    core = lax.rem(index, CORES)
    chip = lax.div(index, CORES)
    copies = []

    def put(source, chip_of, core_of, sem):
        at = pl.multiple_of((chip_of * CORES + core_of) * clips, clips)
        copy = pltpu.make_async_copy(source, out_ref.at[:, pl.ds(at, clips)], sem)
        copy.start()
        copies.append(copy)

    put(mine_ref.at[0], chip, core, sems.at[0])
    put(got_ref.at[0], chip, 1 - core, sems.at[1])
    for j, (ref, flip) in enumerate(((a_ref, 1 + core), (b_ref, 2 - core), (d_ref, 3))):
        there = lax.bitwise_xor(chip, flip)
        put(ref.at[0], there, core, sems.at[2 + 2 * j])
        put(ref.at[1], there, 1 - core, sems.at[3 + 2 * j])
    for copy in copies:
        copy.wait()


def place(mine, got, d, a, b):
    _, rows, clips = mine.shape
    return pl.pallas_call(
        place_kernel,
        out_shape=jax.ShapeDtypeStruct((rows, 8 * clips), F32),
        in_specs=[VMEM] * 5,
        out_specs=HBM,
        scratch_shapes=[pltpu.SemaphoreType.DMA((8,))],
        compiler_params=pltpu.CompilerParams(vmem_limit_bytes=8 << 20),
    )(mine, got, d, a, b)


def per_device_exchanged(planes, queries, block_ids, left_factor, right_factor, clip_grads, lengths):
    size = 4 * CORES

    def move(x, to):
        return lax.ppermute(x, "own", [(i, to(i // CORES, i % CORES)) for i in range(size)])

    def sibling(x):
        return move(x, lambda chip, core: chip * CORES + 1 - core)

    def across(x, flips):
        return move(x, lambda chip, core: (chip ^ flips[core]) * CORES + core)

    flips_a, flips_b, flips_d = (1, 2), (2, 1), (3, 3)
    row, fac = pack(queries[0], block_ids, left_factor, right_factor)
    slot_d = across(row, flips_d)
    slot_a = across(row, flips_a)
    slot_b = across(row, flips_b)
    factors = [fac]
    held = fac
    step = 1
    while step < planes:
        got = lax.ppermute(held, "qry", [(i, i ^ step) for i in range(planes)])
        factors.append(got)
        if step * 2 < planes:
            held = jnp.concatenate([held, got])
        step *= 2
    own = [row, slot_a, slot_b, slot_d]
    slots = own + [sibling(x) for x in own]
    order_a, order_b = left_factor.shape[2], right_factor.shape[2]
    left_all, right_all = place_factors(factors, order_a, order_b)
    mine, other = score(slots, left_all, right_all, clip_grads, lengths, order_a, order_b)
    got = sibling(other)
    back = [
        across(jnp.stack([mine[j], got[j]]), flips) for j, flips in ((3, flips_d), (1, flips_a), (2, flips_b))
    ]
    return place(mine, got, *back)[None]


def solution(mesh):
    owners, planes = mesh.shape["own"], mesh.shape["qry"]

    def per_device(queries, block_ids, left_factor, right_factor, clip_grads, lengths):
        whole_tiles = left_factor.shape[1] % 16 == 0 and right_factor.shape[1] % 16 == 0
        if owners == 4 * CORES and planes & (planes - 1) == 0 and whole_tiles:
            return per_device_exchanged(
                planes, queries, block_ids, left_factor, right_factor, clip_grads, lengths
            )
        return per_device_gathered(queries, block_ids, left_factor, right_factor, clip_grads, lengths)

    in_specs = (
        P("qry", "own", None),
        P("qry", "own"),
        P(None, "qry", None),
        P(None, "qry", None),
        P("own", None),
        P("own"),
    )
    out_specs = P("qry", "own", None)
    return jax.shard_map(
        per_device, mesh=mesh, in_specs=in_specs, out_specs=out_specs, check_vma=False
    )
```

```python
import jax
import jax.numpy as jnp
from jax import lax
from jax.experimental import pallas as pl
from jax.experimental.pallas import tpu as pltpu
from jax.sharding import PartitionSpec as P

LANES = 128
CORES = 2
HEAD = 256
SOME_VMEM = 16 << 20
VMEM = pl.BlockSpec(memory_space=pltpu.VMEM)
HBM = pl.BlockSpec(memory_space=pltpu.HBM)
ANY = pl.BlockSpec(memory_space=pl.ANY)
F32 = jnp.float32
BF16 = jnp.bfloat16


def precondition(rows, id_values, left_full, right_full):
    blocks = left_full.shape[0]
    order_a = left_full.shape[1]
    order_b = right_full.shape[1]
    labels = jnp.arange(blocks)
    onehot = (id_values[:, :, None] == labels[None, None, :]).astype(F32)
    left_rows = jnp.einsum("srk,kac->srac", onehot, left_full.astype(F32), precision=lax.Precision.HIGHEST)
    right_rows = jnp.einsum("srk,kde->srde", onehot, right_full.astype(F32), precision=lax.Precision.HIGHEST)
    matrix = rows.reshape(rows.shape[0], rows.shape[1], order_a, order_b).astype(F32)
    inner = jnp.einsum("srac,srcd->srad", left_rows, matrix, precision=lax.Precision.HIGHEST)
    outer = jnp.einsum("srad,srde->srae", inner, right_rows, precision=lax.Precision.HIGHEST)
    return outer.reshape(rows.shape).astype(BF16)


def per_device_gathered(queries, block_ids, left_factor, right_factor, clip_grads, lengths):
    left_full = lax.all_gather(left_factor, "qry", axis=1, tiled=True)
    right_full = lax.all_gather(right_factor, "qry", axis=1, tiled=True)
    prepared = precondition(queries, block_ids, left_full, right_full)
    tiles = jnp.einsum(
        "srw,cw->src",
        lax.all_gather(prepared, "own", axis=1, tiled=True),
        clip_grads,
        preferred_element_type=F32,
    )
    factor = lax.rsqrt(F32(queries.shape[2]) * lengths.astype(F32))
    return lax.all_to_all(tiles * factor[None, None, :], "own", split_axis=1, concat_axis=2, tiled=True)


def pack_kernel(q_hbm, ids_hbm, left_hbm, right_hbm, row_ref, again_ref, fac_ref, ids_s, left_s, right_s, sems):
    rows, width = q_hbm.shape
    blocks, cut, order_a = left_s.shape
    copies = [
        pltpu.make_async_copy(left_hbm, left_s, sems.at[0]),
        pltpu.make_async_copy(right_hbm, right_s, sems.at[1]),
        pltpu.make_async_copy(ids_hbm, ids_s, sems.at[2]),
        pltpu.make_async_copy(q_hbm, row_ref.at[:, :width], sems.at[3]),
        pltpu.make_async_copy(q_hbm, again_ref.at[:, :width], sems.at[4]),
    ]
    for copy in copies:
        copy.start()
    copies[2].wait()
    square = (rows, rows)
    diagonal = lax.broadcasted_iota(jnp.int32, square, 0) == lax.broadcasted_iota(jnp.int32, square, 1)
    labels = jnp.where(diagonal, jnp.broadcast_to(ids_s[...].astype(F32), square), 0.0)
    column = jnp.sum(labels, axis=1, keepdims=True)
    column = jnp.broadcast_to(column, (rows, LANES)).astype(BF16)
    row_ref[:, width:] = column
    again_ref[:, width:] = column
    copies[0].wait()
    copies[1].wait()
    fac_ref[0, :, :cut, :order_a] = left_s[...]
    fac_ref[0, :, :cut, order_a:] = jnp.zeros((blocks, cut, LANES - order_a), BF16)
    fac_ref[0, :, cut:, :] = right_s[...]
    copies[3].wait()
    copies[4].wait()


def pack(queries, block_ids, left, right):
    rows, width = queries.shape
    blocks, cut = left.shape[:2]
    depth = cut + right.shape[1]
    return pl.pallas_call(
        pack_kernel,
        out_shape=(
            jax.ShapeDtypeStruct((rows, width + LANES), BF16),
            jax.ShapeDtypeStruct((rows, width + LANES), BF16),
            jax.ShapeDtypeStruct((1, blocks, depth, LANES), BF16),
        ),
        in_specs=[HBM] * 4,
        out_specs=(VMEM,) * 3,
        scratch_shapes=[
            pltpu.VMEM(block_ids.shape, block_ids.dtype),
            pltpu.VMEM(left.shape, left.dtype),
            pltpu.VMEM(right.shape, right.dtype),
            pltpu.SemaphoreType.DMA((5,)),
        ],
        compiler_params=pltpu.CompilerParams(vmem_limit_bytes=SOME_VMEM),
    )(*(pltpu.with_memory_space_constraint(x, pltpu.HBM) for x in (queries, block_ids, left, right)))


def prepare(slots, left_all, right_all, in_s, out_s, prep_ref):
    rows = slots[0].shape[0]
    order_a = left_all.shape[1]
    blocks = left_all.shape[0] // order_a
    order_b = right_all.shape[1] // blocks
    width = order_a * order_b
    pair = 2 * rows
    for group in range(len(slots) // 2):
        for half in range(2):
            ref = slots[2 * group + half]
            for a in range(order_a):
                in_s[a * pair + half * rows : a * pair + half * rows + rows, :] = ref[
                    :, a * order_b : (a + 1) * order_b
                ].astype(F32)
        for n in range(0, pair, 2):
            ref = slots[2 * group + n // rows]
            x = jnp.concatenate(
                [in_s[pl.ds(n + j, order_a, stride=pair), :].astype(BF16) for j in range(2)], axis=1
            )
            inner = jnp.dot(left_all, x, preferred_element_type=F32)
            split = []
            ids = []
            for j in range(2):
                label = ref[(n + j) % rows : (n + j) % rows + 1, width:].astype(F32)
                ids.append(label)
                one = inner[:order_a, j * order_b : (j + 1) * order_b]
                for k in range(1, blocks):
                    one = jnp.where(
                        label > k - 0.5,
                        inner[k * order_a : (k + 1) * order_a, j * order_b : (j + 1) * order_b],
                        one,
                    )
                high = one.astype(BF16)
                low = (one - high.astype(F32)).astype(BF16)
                split.append(jnp.concatenate([high, low], axis=1))
            outer = jnp.dot(jnp.concatenate(split, axis=0), right_all, preferred_element_type=F32)
            for j in range(2):
                one = outer[j * order_a : (j + 1) * order_a, :order_b]
                for k in range(1, blocks):
                    one = jnp.where(
                        ids[j] > k - 0.5,
                        outer[j * order_a : (j + 1) * order_a, k * order_b : (k + 1) * order_b],
                        one,
                    )
                out_s[pl.ds(n + j, order_a, stride=pair), :] = one
        for a in range(order_a):
            prep_ref[group * pair : (group + 1) * pair, a * order_b : (a + 1) * order_b] = out_s[
                a * pair : (a + 1) * pair, :
            ].astype(BF16)


def factor_kernel(order_a, order_b, steps, *refs):
    fac_refs = refs[: steps + 1]
    left_ref, right_ref = refs[steps + 1 :]
    blocks = fac_refs[0].shape[1]
    planes = 2**steps
    cut_a, cut_b = order_a // planes, order_b // planes
    plane = lax.axis_index("qry")
    for m in range(planes):
        step = m.bit_length()
        piece = fac_refs[step][m - (1 << (step - 1)) if step else 0]
        at = lax.bitwise_xor(plane, m)
        for k in range(blocks):
            left_ref[pl.ds(pl.multiple_of(k * order_a + at * cut_a, 16), cut_a), :] = piece[k, :cut_a, :order_a]
            for half in range(2):
                right_ref[
                    pl.ds(pl.multiple_of(half * order_b + at * cut_b, 16), cut_b),
                    k * order_b : (k + 1) * order_b,
                ] = piece[k, cut_a:, :]


def place_factors(factors, order_a, order_b):
    blocks = factors[0].shape[1]
    return pl.pallas_call(
        lambda *refs: factor_kernel(order_a, order_b, len(factors) - 1, *refs),
        out_shape=(
            jax.ShapeDtypeStruct((blocks * order_a, order_a), BF16),
            jax.ShapeDtypeStruct((2 * order_b, blocks * order_b), BF16),
        ),
        in_specs=[VMEM] * len(factors),
        out_specs=(VMEM, VMEM),
        compiler_params=pltpu.CompilerParams(vmem_limit_bytes=8 << 20),
        cost_estimate=pl.CostEstimate(flops=10**10, bytes_accessed=10**6, transcendentals=0),
    )(*factors)


def early_kernel(nslots, *refs):
    slots = refs[:nslots]
    left_ref, right_ref, prep_ref, in_s, out_s = refs[nslots:]
    prepare(slots, left_ref[...], right_ref[...], in_s, out_s, prep_ref)


def early(slots, left_all, right_all, order_a, order_b):
    rows = slots[0].shape[0]
    total = len(slots) * rows
    width = order_a * order_b
    return pl.pallas_call(
        lambda *refs: early_kernel(len(slots), *refs),
        out_shape=jax.ShapeDtypeStruct((total, width), BF16),
        in_specs=[VMEM] * (len(slots) + 2),
        out_specs=VMEM,
        scratch_shapes=[pltpu.VMEM((order_a * 2 * rows, order_b), F32)] * 2,
        compiler_params=pltpu.CompilerParams(vmem_limit_bytes=SOME_VMEM),
        cost_estimate=pl.CostEstimate(flops=8 * total * width * order_b, bytes_accessed=4 * total * width, transcendentals=0),
    )(*slots, left_all, right_all)


def score_kernel(nslots, *refs):
    slots = refs[:nslots]
    early_ref, left_ref, right_ref, clips_ref, len_ref = refs[nslots : nslots + 5]
    home_ref, near_ref, x_ref, cross_ref, y_ref, d_ref, in_s, out_s, prep_s, all_s = refs[nslots + 5 :]
    width = clips_ref.shape[1]
    rows = slots[0].shape[0]
    prepare(slots, left_ref[...], right_ref[...], in_s, out_s, prep_s)
    queries = jnp.concatenate([early_ref[...], prep_s[...]], axis=0)
    raw = lax.dot_general(clips_ref[...], queries, (((1,), (1,)), ((), ())), preferred_element_type=F32)
    factor = lax.rsqrt(F32(width) * len_ref[...].astype(F32))
    scores = raw.T * factor
    core = lax.rem(lax.axis_index("own"), CORES)
    for j, (mine, other) in enumerate(((0, 0), (3, 3), (1 + core, 2 - core), (2 - core, 1 + core))):
        at = 2 * j * rows
        all_s[mine, core] = scores[at : at + rows].astype(BF16)
        all_s[other, 1 - core] = scores[at + rows : at + 2 * rows].astype(BF16)
    home_ref[...] = scores[:rows]
    near_ref[...] = all_s[0, 1 - core]
    x_ref[...] = all_s[1, core]
    cross_ref[...] = all_s[1, 1 - core]
    y_ref[...] = all_s[2]
    d_ref[...] = all_s[3]


def score(slots, prepared, left_all, right_all, clip_grads, lengths):
    rows = slots[0].shape[0]
    clips, width = clip_grads.shape
    order_a = left_all.shape[1]
    total = prepared.shape[0] + len(slots) * rows
    return pl.pallas_call(
        lambda *refs: score_kernel(len(slots), *refs),
        out_shape=(
            jax.ShapeDtypeStruct((rows, clips), F32),
            *(jax.ShapeDtypeStruct((rows, clips), BF16),) * 3,
            *(jax.ShapeDtypeStruct((2, rows, clips), BF16),) * 2,
        ),
        in_specs=[VMEM] * (len(slots) + 5),
        out_specs=(VMEM,) * 6,
        scratch_shapes=[pltpu.VMEM((order_a * 2 * rows, width // order_a), F32)] * 2
        + [pltpu.VMEM((len(slots) * rows, width), BF16), pltpu.VMEM((4, 2, rows, clips), BF16)],
        compiler_params=pltpu.CompilerParams(vmem_limit_bytes=SOME_VMEM),
        cost_estimate=pl.CostEstimate(
            flops=2 * total * width * (clips + 1000), bytes_accessed=clips * width * 2, transcendentals=0
        ),
    )(*slots, prepared, left_all, right_all, clip_grads, lengths.reshape(1, clips))


def in_hbm(x):
    return pltpu.with_memory_space_constraint(x, pltpu.HBM)


def join_kernel(first_ref, second_ref, row_ref, both_ref, same_ref):
    del row_ref, same_ref
    count = first_ref.shape[0]
    both_ref[:count] = first_ref[...]
    both_ref[count:] = second_ref[...]


def join(first, second, row):
    return pl.pallas_call(
        join_kernel,
        out_shape=(
            jax.ShapeDtypeStruct((2 * first.shape[0],) + first.shape[1:], first.dtype),
            jax.ShapeDtypeStruct(row.shape, row.dtype),
        ),
        in_specs=[VMEM, VMEM, ANY],
        out_specs=(VMEM, ANY),
        input_output_aliases={2: 1},
        compiler_params=pltpu.CompilerParams(vmem_limit_bytes=8 << 20),
    )(first, second, row)


def relay_kernel(d_ref, y_ref, near_ref, out_ref):
    other = 1 - lax.rem(lax.axis_index("own"), CORES)
    out_ref[0] = d_ref[other]
    out_ref[1] = y_ref[other]
    out_ref[2] = near_ref[...]


def relay(d, y, near):
    return pl.pallas_call(
        relay_kernel,
        out_shape=jax.ShapeDtypeStruct((3,) + near.shape, near.dtype),
        in_specs=[VMEM] * 3,
        out_specs=VMEM,
        compiler_params=pltpu.CompilerParams(vmem_limit_bytes=8 << 20),
    )(d, y, near)


def widen_kernel(home_ref, x_ref, cross_ref, out_ref):
    for j, ref in enumerate((home_ref, x_ref, cross_ref)):
        out_ref[j] = ref[...].astype(F32)


def widen(*parts):
    return pl.pallas_call(
        widen_kernel,
        out_shape=jax.ShapeDtypeStruct((len(parts),) + parts[0].shape, F32),
        in_specs=[VMEM] * len(parts),
        out_specs=VMEM,
        compiler_params=pltpu.CompilerParams(vmem_limit_bytes=8 << 20),
        cost_estimate=pl.CostEstimate(flops=10**10, bytes_accessed=10**6, transcendentals=0),
    )(*parts)


def place_kernel(wide_ref, d_ref, y_ref, relayed_ref, out_ref, wide_s, sem):
    _, rows, clips = wide_ref.shape
    index = lax.axis_index("own")
    core = lax.rem(index, CORES)
    chip = lax.div(index, CORES)

    def put(value, flip, core_of):
        at = pl.multiple_of((lax.bitwise_xor(chip, flip) * CORES + core_of) * clips, clips)
        wide_s[:, pl.ds(at, clips)] = value.astype(F32)

    put(wide_ref[0], 0, core)
    put(wide_ref[1], 1, core)
    put(wide_ref[2], 1, 1 - core)
    put(y_ref[core], 2, core)
    put(d_ref[core], 3, core)
    put(relayed_ref[0], 3, 1 - core)
    put(relayed_ref[1], 2, 1 - core)
    put(relayed_ref[2], 0, 1 - core)
    copy = pltpu.make_async_copy(wide_s, out_ref, sem)
    copy.start()
    copy.wait()


def place(*parts):
    rows, clips = parts[0].shape[1:]
    wide = (rows, 8 * clips)
    return pl.pallas_call(
        place_kernel,
        out_shape=jax.ShapeDtypeStruct(wide, F32),
        in_specs=[VMEM] * len(parts),
        out_specs=HBM,
        scratch_shapes=[pltpu.VMEM(wide, F32), pltpu.SemaphoreType.DMA(())],
        compiler_params=pltpu.CompilerParams(vmem_limit_bytes=8 << 20),
    )(*parts)


def per_device_exchanged(planes, queries, block_ids, left_factor, right_factor, clip_grads, lengths):
    size = 4 * CORES

    def move(x, to):
        return lax.ppermute(x, "own", [(i, to(i // CORES, i % CORES)) for i in range(size)])

    def sibling(x):
        return move(x, lambda chip, core: chip * CORES + 1 - core)

    def across(x, flips):
        return move(x, lambda chip, core: (chip ^ flips[core]) * CORES + core)

    flips_a, flips_b = (1, 2), (2, 1)
    row, again, fac = pack(queries[0], block_ids, left_factor, right_factor)
    slot_d = across(row, (3, 3))
    slot_a = across(row, flips_a)
    factors = [fac]
    held = fac
    step = 1
    while step < planes:
        got = lax.ppermute(held, "qry", [(i, i ^ step) for i in range(planes)])
        factors.append(got)
        if step * 2 < planes:
            held, again = join(held, got, again)
        step *= 2
    slot_b = across(again, flips_b)
    order_a, order_b = left_factor.shape[2], right_factor.shape[2]
    left_all, right_all = place_factors(factors, order_a, order_b)
    prepared = early(
        [row, sibling(row), slot_d, sibling(slot_d)], left_all, right_all, order_a, order_b
    )
    home, near, x, cross, y, d = score([slot_a, sibling(slot_a), slot_b, sibling(slot_b)], prepared, left_all, right_all, clip_grads, lengths)
    y, d = across(y, (2, 2)), across(d, (3, 3))
    x, cross = across(x, (1, 1)), move(cross, lambda chip, core: (chip ^ 1) * CORES + 1 - core)
    return place(widen(home, x, cross), d, y, sibling(relay(d, y, near)))[None]


def solution(mesh):
    owners, planes = mesh.shape["own"], mesh.shape["qry"]

    def per_device(queries, block_ids, left_factor, right_factor, clip_grads, lengths):
        whole_tiles = left_factor.shape[1] % 16 == 0 and right_factor.shape[1] % 16 == 0
        if owners == 4 * CORES and planes & (planes - 1) == 0 and whole_tiles:
            return per_device_exchanged(
                planes, queries, block_ids, left_factor, right_factor, clip_grads, lengths
            )
        return per_device_gathered(queries, block_ids, left_factor, right_factor, clip_grads, lengths)

    in_specs = (
        P("qry", "own", None),
        P("qry", "own"),
        P(None, "qry", None),
        P(None, "qry", None),
        P("own", None),
        P("own"),
    )
    out_specs = P("qry", "own", None)
    return jax.shard_map(
        per_device, mesh=mesh, in_specs=in_specs, out_specs=out_specs, check_vma=False
    )
```

```python
import jax
import jax.numpy as jnp
from jax import lax
from jax.experimental import pallas as pl
from jax.experimental.pallas import tpu as pltpu
from jax.sharding import PartitionSpec as P

LANES = 128
CORES = 2
HEAD = 256
SOME_VMEM = 16 << 20
VMEM = pl.BlockSpec(memory_space=pltpu.VMEM)
HBM = pl.BlockSpec(memory_space=pltpu.HBM)
ANY = pl.BlockSpec(memory_space=pl.ANY)
F32 = jnp.float32
BF16 = jnp.bfloat16


def precondition(rows, id_values, left_full, right_full):
    blocks = left_full.shape[0]
    order_a = left_full.shape[1]
    order_b = right_full.shape[1]
    labels = jnp.arange(blocks)
    onehot = (id_values[:, :, None] == labels[None, None, :]).astype(F32)
    left_rows = jnp.einsum("srk,kac->srac", onehot, left_full.astype(F32), precision=lax.Precision.HIGHEST)
    right_rows = jnp.einsum("srk,kde->srde", onehot, right_full.astype(F32), precision=lax.Precision.HIGHEST)
    matrix = rows.reshape(rows.shape[0], rows.shape[1], order_a, order_b).astype(F32)
    inner = jnp.einsum("srac,srcd->srad", left_rows, matrix, precision=lax.Precision.HIGHEST)
    outer = jnp.einsum("srad,srde->srae", inner, right_rows, precision=lax.Precision.HIGHEST)
    return outer.reshape(rows.shape).astype(BF16)


def per_device_gathered(queries, block_ids, left_factor, right_factor, clip_grads, lengths):
    left_full = lax.all_gather(left_factor, "qry", axis=1, tiled=True)
    right_full = lax.all_gather(right_factor, "qry", axis=1, tiled=True)
    prepared = precondition(queries, block_ids, left_full, right_full)
    tiles = jnp.einsum(
        "srw,cw->src",
        lax.all_gather(prepared, "own", axis=1, tiled=True),
        clip_grads,
        preferred_element_type=F32,
    )
    factor = lax.rsqrt(F32(queries.shape[2]) * lengths.astype(F32))
    return lax.all_to_all(tiles * factor[None, None, :], "own", split_axis=1, concat_axis=2, tiled=True)


def pack_kernel(q_hbm, ids_hbm, left_hbm, right_hbm, row_ref, again_ref, fac_ref, ids_s, left_s, right_s, sems):
    rows, width = q_hbm.shape
    blocks, cut, order_a = left_s.shape
    copies = [
        pltpu.make_async_copy(left_hbm, left_s, sems.at[0]),
        pltpu.make_async_copy(right_hbm, right_s, sems.at[1]),
        pltpu.make_async_copy(ids_hbm, ids_s, sems.at[2]),
        pltpu.make_async_copy(q_hbm, row_ref.at[:, :width], sems.at[3]),
        pltpu.make_async_copy(q_hbm, again_ref.at[:, :width], sems.at[4]),
    ]
    for copy in copies[::-1]:
        copy.start()
    copies[2].wait()
    square = (rows, rows)
    diagonal = lax.broadcasted_iota(jnp.int32, square, 0) == lax.broadcasted_iota(jnp.int32, square, 1)
    labels = jnp.where(diagonal, jnp.broadcast_to(ids_s[...].astype(F32), square), 0.0)
    column = jnp.sum(labels, axis=1, keepdims=True)
    column = jnp.broadcast_to(column, (rows, LANES)).astype(BF16)
    row_ref[:, width:] = column
    again_ref[:, width:] = column
    copies[0].wait()
    copies[1].wait()
    fac_ref[0, :, :cut, :order_a] = left_s[...]
    fac_ref[0, :, :cut, order_a:] = jnp.zeros((blocks, cut, LANES - order_a), BF16)
    fac_ref[0, :, cut:, :] = right_s[...]
    copies[3].wait()
    copies[4].wait()


def pack(queries, block_ids, left, right):
    rows, width = queries.shape
    blocks, cut = left.shape[:2]
    depth = cut + right.shape[1]
    return pl.pallas_call(
        pack_kernel,
        out_shape=(
            jax.ShapeDtypeStruct((rows, width + LANES), BF16),
            jax.ShapeDtypeStruct((rows, width + LANES), BF16),
            jax.ShapeDtypeStruct((1, blocks, depth, LANES), BF16),
        ),
        in_specs=[HBM] * 4,
        out_specs=(VMEM,) * 3,
        scratch_shapes=[
            pltpu.VMEM(block_ids.shape, block_ids.dtype),
            pltpu.VMEM(left.shape, left.dtype),
            pltpu.VMEM(right.shape, right.dtype),
            pltpu.SemaphoreType.DMA((5,)),
        ],
        compiler_params=pltpu.CompilerParams(vmem_limit_bytes=SOME_VMEM),
    )(*(pltpu.with_memory_space_constraint(x, pltpu.HBM) for x in (queries, block_ids, left, right)))


def prepare(slots, left_all, right_all, in_s, mid_s, out_s, prep_ref):
    rows = slots[0].shape[0]
    order_a = left_all.shape[1]
    blocks = left_all.shape[0] // order_a
    order_b = right_all.shape[1] // blocks
    width = order_a * order_b
    pair = 2 * rows

    def label_of(group, n):
        row = slots[2 * group + n // rows][n % rows : n % rows + 1, width:]
        return row.astype(F32)

    for group in range(len(slots) // 2):
        both = slots[2 * group : 2 * group + 2]
        tiles = [
            jnp.concatenate([ref[:, a * order_b : (a + 1) * order_b] for ref in both], axis=0) for a in range(order_a)
        ]
        in_s[group] = jnp.swapaxes(jnp.stack(tiles), 0, 1)
    for group in range(len(slots) // 2):
        for n in range(0, pair, 2):
            x = jnp.concatenate([in_s[group, n + j] for j in range(2)], axis=1)
            inner = jnp.dot(left_all, x, preferred_element_type=F32)
            for j in range(2):
                label = label_of(group, n + j)
                one = inner[:order_a, j * order_b : (j + 1) * order_b]
                for k in range(1, blocks):
                    one = jnp.where(
                        label > k - 0.5,
                        inner[k * order_a : (k + 1) * order_a, j * order_b : (j + 1) * order_b],
                        one,
                    )
                high = one.astype(BF16)
                mid_s[group, n + j, :, :order_b] = high
                mid_s[group, n + j, :, order_b:] = (one - high.astype(F32)).astype(BF16)
    for group in range(len(slots) // 2):
        middle = mid_s[group].reshape(pair * order_a, 2 * order_b)
        outer = jnp.dot(middle, right_all, preferred_element_type=F32)
        for n in range(pair):
            label = label_of(group, n)
            one = outer[n * order_a : (n + 1) * order_a, :order_b]
            for k in range(1, blocks):
                one = jnp.where(
                    label > k - 0.5, outer[n * order_a : (n + 1) * order_a, k * order_b : (k + 1) * order_b], one
                )
            out_s[group, n] = one.astype(BF16)
    for group in range(len(slots) // 2):
        turned = jnp.swapaxes(out_s[group], 0, 1)
        for a in range(order_a):
            prep_ref[group * pair : (group + 1) * pair, a * order_b : (a + 1) * order_b] = turned[a]


def factor_kernel(order_a, order_b, steps, *refs):
    fac_refs = refs[: steps + 1]
    left_ref, right_ref = refs[steps + 1 :]
    blocks = fac_refs[0].shape[1]
    planes = 2**steps
    cut_a, cut_b = order_a // planes, order_b // planes
    plane = lax.axis_index("qry")
    for m in range(planes):
        step = m.bit_length()
        piece = fac_refs[step][m - (1 << (step - 1)) if step else 0]
        at = lax.bitwise_xor(plane, m)
        for k in range(blocks):
            left_ref[pl.ds(pl.multiple_of(k * order_a + at * cut_a, 16), cut_a), :] = piece[k, :cut_a, :order_a]
            for half in range(2):
                right_ref[
                    pl.ds(pl.multiple_of(half * order_b + at * cut_b, 16), cut_b),
                    k * order_b : (k + 1) * order_b,
                ] = piece[k, cut_a:, :]


def place_factors(factors, order_a, order_b):
    blocks = factors[0].shape[1]
    return pl.pallas_call(
        lambda *refs: factor_kernel(order_a, order_b, len(factors) - 1, *refs),
        out_shape=(
            jax.ShapeDtypeStruct((blocks * order_a, order_a), BF16),
            jax.ShapeDtypeStruct((2 * order_b, blocks * order_b), BF16),
        ),
        in_specs=[VMEM] * len(factors),
        out_specs=(VMEM, VMEM),
        compiler_params=pltpu.CompilerParams(vmem_limit_bytes=8 << 20),
        cost_estimate=pl.CostEstimate(flops=6*10**9, bytes_accessed=10**6, transcendentals=0),
    )(*factors)


def early_kernel(nslots, *refs):
    slots = refs[:nslots]
    left_ref, right_ref, prep_ref, in_s, mid_s, out_s = refs[nslots:]
    prepare(slots, left_ref[...], right_ref[...], in_s, mid_s, out_s, prep_ref)


def early(slots, left_all, right_all, order_a, order_b):
    rows = slots[0].shape[0]
    total = len(slots) * rows
    width = order_a * order_b
    return pl.pallas_call(
        lambda *refs: early_kernel(len(slots), *refs),
        out_shape=jax.ShapeDtypeStruct((total, width), BF16),
        in_specs=[VMEM] * (len(slots) + 2),
        out_specs=VMEM,
        scratch_shapes=[
            pltpu.VMEM((len(slots) // 2, 2 * rows, order_a, wide * order_b), BF16) for wide in (1, 2, 1)
        ],
        compiler_params=pltpu.CompilerParams(vmem_limit_bytes=SOME_VMEM),
        cost_estimate=pl.CostEstimate(flops=8 * total * width * order_b, bytes_accessed=4 * total * width, transcendentals=0),
    )(*slots, left_all, right_all)


def score_kernel(nslots, *refs):
    slots = refs[:nslots]
    early_ref, left_ref, right_ref, clips_ref, len_ref = refs[nslots : nslots + 5]
    home_ref, near_ref, x_ref, cross_ref, y_ref, d_ref, in_s, mid_s, out_s, prep_s, all_s = refs[nslots + 5 :]
    width = clips_ref.shape[1]
    rows = slots[0].shape[0]
    prepare(slots, left_ref[...], right_ref[...], in_s, mid_s, out_s, prep_s)
    @pl.when(lax.axis_index("qry") >= 0)
    def _():
        queries = jnp.concatenate([early_ref[...], prep_s[...]], axis=0)
        raw = lax.dot_general(clips_ref[...], queries, (((1,), (1,)), ((), ())), preferred_element_type=F32)
        factor = lax.rsqrt(F32(width) * len_ref[...].astype(F32))
        scores = raw.T * factor
        core = lax.rem(lax.axis_index("own"), CORES)
        for j, (mine, other) in enumerate(((0, 0), (3, 3), (1 + core, 2 - core), (2 - core, 1 + core))):
            at = 2 * j * rows
            all_s[mine, core] = scores[at : at + rows].astype(BF16)
            all_s[other, 1 - core] = scores[at + rows : at + 2 * rows].astype(BF16)
        home_ref[...] = scores[:rows]
        near_ref[...] = all_s[0, 1 - core]
        x_ref[...] = all_s[1, core]
        cross_ref[...] = all_s[1, 1 - core]
        y_ref[...] = all_s[2]
        d_ref[...] = all_s[3]


def score(slots, prepared, left_all, right_all, clip_grads, lengths):
    rows = slots[0].shape[0]
    clips, width = clip_grads.shape
    order_a = left_all.shape[1]
    total = prepared.shape[0] + len(slots) * rows
    return pl.pallas_call(
        lambda *refs: score_kernel(len(slots), *refs),
        out_shape=(
            jax.ShapeDtypeStruct((rows, clips), F32),
            *(jax.ShapeDtypeStruct((rows, clips), BF16),) * 3,
            *(jax.ShapeDtypeStruct((2, rows, clips), BF16),) * 2,
        ),
        in_specs=[VMEM] * (len(slots) + 5),
        out_specs=(VMEM,) * 6,
        scratch_shapes=[
            pltpu.VMEM((len(slots) // 2, 2 * rows, order_a, wide * width // order_a), BF16) for wide in (1, 2, 1)
        ]
        + [pltpu.VMEM((len(slots) * rows, width), BF16), pltpu.VMEM((4, 2, rows, clips), BF16)],
        compiler_params=pltpu.CompilerParams(vmem_limit_bytes=SOME_VMEM),
        cost_estimate=pl.CostEstimate(
            flops=2 * total * width * (clips + 1000), bytes_accessed=clips * width * 2, transcendentals=0
        ),
    )(*slots, prepared, left_all, right_all, clip_grads, lengths.reshape(1, clips))


def in_hbm(x):
    return pltpu.with_memory_space_constraint(x, pltpu.HBM)


def join_kernel(first_ref, second_ref, row_ref, both_ref, same_ref):
    del row_ref, same_ref
    count = first_ref.shape[0]
    both_ref[:count] = first_ref[...]
    both_ref[count:] = second_ref[...]


def join(first, second, row):
    return pl.pallas_call(
        join_kernel,
        out_shape=(
            jax.ShapeDtypeStruct((2 * first.shape[0],) + first.shape[1:], first.dtype),
            jax.ShapeDtypeStruct(row.shape, row.dtype),
        ),
        in_specs=[VMEM, VMEM, ANY],
        out_specs=(VMEM, ANY),
        input_output_aliases={2: 1},
        compiler_params=pltpu.CompilerParams(vmem_limit_bytes=8 << 20),
    )(first, second, row)


def relay_kernel(d_ref, y_ref, near_ref, out_ref):
    other = 1 - lax.rem(lax.axis_index("own"), CORES)
    out_ref[0] = d_ref[other]
    out_ref[1] = y_ref[other]
    out_ref[2] = near_ref[...]


def relay(d, y, near):
    return pl.pallas_call(
        relay_kernel,
        out_shape=jax.ShapeDtypeStruct((3,) + near.shape, near.dtype),
        in_specs=[VMEM] * 3,
        out_specs=VMEM,
        compiler_params=pltpu.CompilerParams(vmem_limit_bytes=8 << 20),
    )(d, y, near)


def widen_kernel(home_ref, x_ref, cross_ref, out_ref):
    for j, ref in enumerate((home_ref, x_ref, cross_ref)):
        out_ref[j] = ref[...].astype(F32)


def widen(*parts):
    return pl.pallas_call(
        widen_kernel,
        out_shape=jax.ShapeDtypeStruct((len(parts),) + parts[0].shape, F32),
        in_specs=[VMEM] * len(parts),
        out_specs=VMEM,
        compiler_params=pltpu.CompilerParams(vmem_limit_bytes=8 << 20),
        cost_estimate=pl.CostEstimate(flops=10**10, bytes_accessed=10**6, transcendentals=0),
    )(*parts)


def place_kernel(wide_ref, d_ref, y_ref, relayed_ref, out_ref, wide_s, sem):
    _, rows, clips = wide_ref.shape
    index = lax.axis_index("own")
    core = lax.rem(index, CORES)
    chip = lax.div(index, CORES)

    def put(value, flip, core_of):
        at = pl.multiple_of((lax.bitwise_xor(chip, flip) * CORES + core_of) * clips, clips)
        wide_s[:, pl.ds(at, clips)] = value.astype(F32)

    put(wide_ref[0], 0, core)
    put(wide_ref[1], 1, core)
    put(wide_ref[2], 1, 1 - core)
    put(y_ref[core], 2, core)
    put(d_ref[core], 3, core)
    put(relayed_ref[0], 3, 1 - core)
    put(relayed_ref[1], 2, 1 - core)
    put(relayed_ref[2], 0, 1 - core)
    copy = pltpu.make_async_copy(wide_s, out_ref, sem)
    copy.start()
    copy.wait()


def place(*parts):
    rows, clips = parts[0].shape[1:]
    wide = (rows, 8 * clips)
    return pl.pallas_call(
        place_kernel,
        out_shape=jax.ShapeDtypeStruct(wide, F32),
        in_specs=[VMEM] * len(parts),
        out_specs=HBM,
        scratch_shapes=[pltpu.VMEM(wide, F32), pltpu.SemaphoreType.DMA(())],
        compiler_params=pltpu.CompilerParams(vmem_limit_bytes=8 << 20),
    )(*parts)


def per_device_exchanged(planes, queries, block_ids, left_factor, right_factor, clip_grads, lengths):
    size = 4 * CORES

    def move(x, to):
        return lax.ppermute(x, "own", [(i, to(i // CORES, i % CORES)) for i in range(size)])

    def sibling(x):
        return move(x, lambda chip, core: chip * CORES + 1 - core)

    def across(x, flips):
        return move(x, lambda chip, core: (chip ^ flips[core]) * CORES + core)

    flips_a, flips_b = (1, 2), (2, 1)
    row, again, fac = pack(queries[0], block_ids, left_factor, right_factor)
    slot_d = across(row, (3, 3))
    slot_a = across(row, flips_a)
    factors = [fac]
    held = fac
    step = 1
    while step < planes:
        got = lax.ppermute(held, "qry", [(i, i ^ step) for i in range(planes)])
        factors.append(got)
        if step * 2 < planes:
            held, again = join(held, got, again)
        step *= 2
    slot_b = across(again, flips_b)
    order_a, order_b = left_factor.shape[2], right_factor.shape[2]
    left_all, right_all = place_factors(factors, order_a, order_b)
    prepared = early(
        [row, sibling(row), slot_d, sibling(slot_d)], left_all, right_all, order_a, order_b
    )
    home, near, x, cross, y, d = score([slot_a, sibling(slot_a), slot_b, sibling(slot_b)], prepared, left_all, right_all, clip_grads, lengths)
    y, d = across(y, (2, 2)), across(d, (3, 3))
    x, cross = across(x, (1, 1)), move(cross, lambda chip, core: (chip ^ 1) * CORES + 1 - core)
    return place(widen(home, x, cross), d, y, sibling(relay(d, y, near)))[None]


def solution(mesh):
    owners, planes = mesh.shape["own"], mesh.shape["qry"]

    def per_device(queries, block_ids, left_factor, right_factor, clip_grads, lengths):
        whole_tiles = left_factor.shape[1] % 16 == 0 and right_factor.shape[1] % 16 == 0
        if owners == 4 * CORES and planes & (planes - 1) == 0 and whole_tiles:
            return per_device_exchanged(
                planes, queries, block_ids, left_factor, right_factor, clip_grads, lengths
            )
        return per_device_gathered(queries, block_ids, left_factor, right_factor, clip_grads, lengths)

    in_specs = (
        P("qry", "own", None),
        P("qry", "own"),
        P(None, "qry", None),
        P(None, "qry", None),
        P("own", None),
        P("own"),
    )
    out_specs = P("qry", "own", None)
    return jax.shard_map(
        per_device, mesh=mesh, in_specs=in_specs, out_specs=out_specs, check_vma=False
    )
```

```python
import jax
import jax.numpy as jnp
from jax import lax
from jax.experimental import pallas as pl
from jax.experimental.pallas import tpu as pltpu
from jax.sharding import PartitionSpec as P

LANES = 128
CORES = 2
HEAD = 256
SOME_VMEM = 16 << 20
VMEM = pl.BlockSpec(memory_space=pltpu.VMEM)
HBM = pl.BlockSpec(memory_space=pltpu.HBM)
F32 = jnp.float32
BF16 = jnp.bfloat16


def precondition(rows, id_values, left_full, right_full):
    blocks = left_full.shape[0]
    order_a = left_full.shape[1]
    order_b = right_full.shape[1]
    labels = jnp.arange(blocks)
    onehot = (id_values[:, :, None] == labels[None, None, :]).astype(F32)
    left_rows = jnp.einsum("srk,kac->srac", onehot, left_full.astype(F32), precision=lax.Precision.HIGHEST)
    right_rows = jnp.einsum("srk,kde->srde", onehot, right_full.astype(F32), precision=lax.Precision.HIGHEST)
    matrix = rows.reshape(rows.shape[0], rows.shape[1], order_a, order_b).astype(F32)
    inner = jnp.einsum("srac,srcd->srad", left_rows, matrix, precision=lax.Precision.HIGHEST)
    outer = jnp.einsum("srad,srde->srae", inner, right_rows, precision=lax.Precision.HIGHEST)
    return outer.reshape(rows.shape).astype(BF16)


def per_device_gathered(queries, block_ids, left_factor, right_factor, clip_grads, lengths):
    left_full = lax.all_gather(left_factor, "qry", axis=1, tiled=True)
    right_full = lax.all_gather(right_factor, "qry", axis=1, tiled=True)
    prepared = precondition(queries, block_ids, left_full, right_full)
    tiles = jnp.einsum(
        "srw,cw->src",
        lax.all_gather(prepared, "own", axis=1, tiled=True),
        clip_grads,
        preferred_element_type=F32,
    )
    factor = lax.rsqrt(F32(queries.shape[2]) * lengths.astype(F32))
    return lax.all_to_all(tiles * factor[None, None, :], "own", split_axis=1, concat_axis=2, tiled=True)


def pack_kernel(q_hbm, ids_hbm, left_hbm, right_hbm, row_ref, fac_ref, ids_s, left_s, sems):
    rows, width = q_hbm.shape
    blocks, cut, order_a = left_s.shape
    copies = [
        pltpu.make_async_copy(ids_hbm, ids_s, sems.at[1]),
        pltpu.make_async_copy(left_hbm, left_s, sems.at[2]),
        pltpu.make_async_copy(right_hbm, fac_ref.at[0, :, cut:, :], sems.at[3]),
    ]
    part = width // 4
    copies = [
        pltpu.make_async_copy(
            q_hbm.at[:, i * part : (i + 1) * part], row_ref.at[:, i * part : (i + 1) * part], sems.at[4 + i]
        )
        for i in range(4)
    ] + copies
    for copy in copies:
        copy.start()
    fac_ref[0, :, :cut, order_a:] = jnp.zeros((blocks, cut, LANES - order_a), BF16)
    square = (rows, rows)
    diagonal = lax.broadcasted_iota(jnp.int32, square, 0) == lax.broadcasted_iota(jnp.int32, square, 1)
    copies[4].wait()
    labels = jnp.where(diagonal, jnp.broadcast_to(ids_s[...].astype(F32), square), 0.0)
    column = jnp.sum(labels, axis=1, keepdims=True)
    column = jnp.broadcast_to(column, (rows, LANES)).astype(BF16)
    row_ref[:, width:] = column
    copies[5].wait()
    fac_ref[0, :, :cut, :order_a] = left_s[...]
    for copy in copies[:4] + copies[6:]:
        copy.wait()


def pack(queries, block_ids, left, right):
    rows, width = queries.shape
    blocks, cut = left.shape[:2]
    depth = cut + right.shape[1]
    return pl.pallas_call(
        pack_kernel,
        out_shape=(
            jax.ShapeDtypeStruct((rows, width + LANES), BF16),
            jax.ShapeDtypeStruct((1, blocks, depth, LANES), BF16),
        ),
        in_specs=[HBM] * 4,
        out_specs=(VMEM, VMEM),
        scratch_shapes=[
            pltpu.VMEM(block_ids.shape, block_ids.dtype),
            pltpu.VMEM(left.shape, left.dtype),
            pltpu.SemaphoreType.DMA((8,)),
        ],
        compiler_params=pltpu.CompilerParams(vmem_limit_bytes=SOME_VMEM),
    )(*(pltpu.with_memory_space_constraint(x, pltpu.HBM) for x in (queries, block_ids, left, right)))


def prepare(slots, left_all, right_all, in_s, mid_s, out_s, prep_ref):
    rows = slots[0].shape[0]
    order_a = left_all.shape[1]
    blocks = left_all.shape[0] // order_a
    order_b = right_all.shape[1] // blocks
    width = order_a * order_b
    pair = 2 * rows

    def label_of(group, n):
        row = slots[2 * group + n // rows][n % rows : n % rows + 1, width:]
        return row.astype(F32)

    for group in range(len(slots) // 2):
        both = slots[2 * group : 2 * group + 2]
        tiles = [
            jnp.concatenate([ref[:, a * order_b : (a + 1) * order_b] for ref in both], axis=0) for a in range(order_a)
        ]
        in_s[group] = jnp.swapaxes(jnp.stack(tiles), 0, 1)
    for group in range(len(slots) // 2):
        for n in range(0, pair, 2):
            x = jnp.concatenate([in_s[group, n + j] for j in range(2)], axis=1)
            inner = jnp.dot(left_all, x, preferred_element_type=F32)
            for j in range(2):
                label = label_of(group, n + j)
                one = inner[:order_a, j * order_b : (j + 1) * order_b]
                for k in range(1, blocks):
                    one = jnp.where(
                        label > k - 0.5,
                        inner[k * order_a : (k + 1) * order_a, j * order_b : (j + 1) * order_b],
                        one,
                    )
                high = one.astype(BF16)
                mid_s[group, n + j, :, :order_b] = high
                mid_s[group, n + j, :, order_b:] = (one - high.astype(F32)).astype(BF16)
    for group in range(len(slots) // 2):
        middle = mid_s[group].reshape(pair * order_a, 2 * order_b)
        outer = jnp.dot(middle, right_all, preferred_element_type=F32)
        for n in range(pair):
            label = label_of(group, n)
            one = outer[n * order_a : (n + 1) * order_a, :order_b]
            for k in range(1, blocks):
                one = jnp.where(
                    label > k - 0.5, outer[n * order_a : (n + 1) * order_a, k * order_b : (k + 1) * order_b], one
                )
            out_s[group, n] = one.astype(BF16)
    for group in range(len(slots) // 2):
        turned = jnp.swapaxes(out_s[group], 0, 1)
        for a in range(order_a):
            prep_ref[group * pair : (group + 1) * pair, a * order_b : (a + 1) * order_b] = turned[a]


def factor_kernel(order_a, order_b, steps, *refs):
    fac_refs = refs[: steps + 1]
    left_ref, right_ref = refs[steps + 1 :]
    blocks = fac_refs[0].shape[1]
    planes = 2**steps
    cut_a, cut_b = order_a // planes, order_b // planes
    plane = lax.axis_index("qry")
    for m in range(planes):
        step = m.bit_length()
        piece = fac_refs[step][m - (1 << (step - 1)) if step else 0]
        at = lax.bitwise_xor(plane, m)
        for k in range(blocks):
            left_ref[pl.ds(pl.multiple_of(k * order_a + at * cut_a, 16), cut_a), :] = piece[k, :cut_a, :order_a]
            for half in range(2):
                right_ref[
                    pl.ds(pl.multiple_of(half * order_b + at * cut_b, 16), cut_b),
                    k * order_b : (k + 1) * order_b,
                ] = piece[k, cut_a:, :]


def place_factors(factors, order_a, order_b):
    blocks = factors[0].shape[1]
    return pl.pallas_call(
        lambda *refs: factor_kernel(order_a, order_b, len(factors) - 1, *refs),
        out_shape=(
            jax.ShapeDtypeStruct((blocks * order_a, order_a), BF16),
            jax.ShapeDtypeStruct((2 * order_b, blocks * order_b), BF16),
        ),
        in_specs=[VMEM] * len(factors),
        out_specs=(VMEM, VMEM),
        compiler_params=pltpu.CompilerParams(vmem_limit_bytes=8 << 20),
        cost_estimate=pl.CostEstimate(flops=6*10**9, bytes_accessed=10**6, transcendentals=0),
    )(*factors)


def early_kernel(nslots, *refs):
    slots = refs[:nslots]
    left_ref, right_ref, prep_ref, in_s, mid_s, out_s = refs[nslots:]
    prepare(slots, left_ref[...], right_ref[...], in_s, mid_s, out_s, prep_ref)


def early(slots, left_all, right_all, order_a, order_b):
    rows = slots[0].shape[0]
    total = len(slots) * rows
    width = order_a * order_b
    return pl.pallas_call(
        lambda *refs: early_kernel(len(slots), *refs),
        out_shape=jax.ShapeDtypeStruct((total, width), BF16),
        in_specs=[VMEM] * (len(slots) + 2),
        out_specs=VMEM,
        scratch_shapes=[
            pltpu.VMEM((len(slots) // 2, 2 * rows, order_a, wide * order_b), BF16) for wide in (1, 2, 1)
        ],
        compiler_params=pltpu.CompilerParams(vmem_limit_bytes=SOME_VMEM),
        cost_estimate=pl.CostEstimate(flops=8 * total * width * order_b, bytes_accessed=4 * total * width, transcendentals=0),
    )(*slots, left_all, right_all)


def score_kernel(nslots, *refs):
    slots = refs[:nslots]
    early_ref, left_ref, right_ref, clips_ref, len_ref = refs[nslots : nslots + 5]
    home_ref, near_ref, x_ref, cross_ref, y_ref, d_ref, in_s, mid_s, out_s, prep_s, all_s = refs[nslots + 5 :]
    width = clips_ref.shape[1]
    rows = slots[0].shape[0]
    prepare(slots, left_ref[...], right_ref[...], in_s, mid_s, out_s, prep_s)
    @pl.when(lax.axis_index("qry") >= 0)
    def _():
        queries = jnp.concatenate([early_ref[...], prep_s[...]], axis=0)
        raw = lax.dot_general(clips_ref[...], queries, (((1,), (1,)), ((), ())), preferred_element_type=F32)
        factor = lax.rsqrt(F32(width) * len_ref[...].astype(F32))
        scores = raw.T * factor
        core = lax.rem(lax.axis_index("own"), CORES)
        for j, (mine, other) in enumerate(((0, 0), (3, 3), (1 + core, 2 - core), (2 - core, 1 + core))):
            at = 2 * j * rows
            all_s[mine, core] = scores[at : at + rows].astype(BF16)
            all_s[other, 1 - core] = scores[at + rows : at + 2 * rows].astype(BF16)
        home_ref[...] = scores[:rows]
        near_ref[...] = all_s[0, 1 - core]
        x_ref[...] = all_s[1, core]
        cross_ref[...] = all_s[1, 1 - core]
        y_ref[...] = all_s[2]
        d_ref[...] = all_s[3]


def score(slots, prepared, left_all, right_all, clip_grads, lengths):
    rows = slots[0].shape[0]
    clips, width = clip_grads.shape
    order_a = left_all.shape[1]
    total = prepared.shape[0] + len(slots) * rows
    return pl.pallas_call(
        lambda *refs: score_kernel(len(slots), *refs),
        out_shape=(
            jax.ShapeDtypeStruct((rows, clips), F32),
            *(jax.ShapeDtypeStruct((rows, clips), BF16),) * 3,
            *(jax.ShapeDtypeStruct((2, rows, clips), BF16),) * 2,
        ),
        in_specs=[VMEM] * (len(slots) + 5),
        out_specs=(VMEM,) * 6,
        scratch_shapes=[
            pltpu.VMEM((len(slots) // 2, 2 * rows, order_a, wide * width // order_a), BF16) for wide in (1, 2, 1)
        ]
        + [pltpu.VMEM((len(slots) * rows, width), BF16), pltpu.VMEM((4, 2, rows, clips), BF16)],
        compiler_params=pltpu.CompilerParams(vmem_limit_bytes=SOME_VMEM),
        cost_estimate=pl.CostEstimate(
            flops=2 * total * width * (clips + 1000), bytes_accessed=clips * width * 2, transcendentals=0
        ),
    )(*slots, prepared, left_all, right_all, clip_grads, lengths.reshape(1, clips))


def in_hbm(x):
    return pltpu.with_memory_space_constraint(x, pltpu.HBM)


def join_kernel(first_ref, second_ref, row_ref, both_ref, again_ref):
    count = first_ref.shape[0]
    both_ref[:count] = first_ref[...]
    both_ref[count:] = second_ref[...]
    again_ref[...] = row_ref[...]


def join(first, second, row):
    return pl.pallas_call(
        join_kernel,
        out_shape=(
            jax.ShapeDtypeStruct((2 * first.shape[0],) + first.shape[1:], first.dtype),
            jax.ShapeDtypeStruct(row.shape, row.dtype),
        ),
        in_specs=[VMEM] * 3,
        out_specs=(VMEM, VMEM),
        compiler_params=pltpu.CompilerParams(vmem_limit_bytes=8 << 20),
    )(first, second, row)


def relay_kernel(d_ref, y_ref, near_ref, out_ref):
    other = 1 - lax.rem(lax.axis_index("own"), CORES)
    out_ref[0] = d_ref[other]
    out_ref[1] = y_ref[other]
    out_ref[2] = near_ref[...]


def relay(d, y, near):
    return pl.pallas_call(
        relay_kernel,
        out_shape=jax.ShapeDtypeStruct((3,) + near.shape, near.dtype),
        in_specs=[VMEM] * 3,
        out_specs=VMEM,
        compiler_params=pltpu.CompilerParams(vmem_limit_bytes=8 << 20),
    )(d, y, near)


def widen_kernel(home_ref, x_ref, cross_ref, out_ref):
    for j, ref in enumerate((home_ref, x_ref, cross_ref)):
        out_ref[j] = ref[...].astype(F32)


def widen(*parts):
    return pl.pallas_call(
        widen_kernel,
        out_shape=jax.ShapeDtypeStruct((len(parts),) + parts[0].shape, F32),
        in_specs=[VMEM] * len(parts),
        out_specs=VMEM,
        compiler_params=pltpu.CompilerParams(vmem_limit_bytes=8 << 20),
        cost_estimate=pl.CostEstimate(flops=10**10, bytes_accessed=10**6, transcendentals=0),
    )(*parts)


def place_kernel(wide_ref, d_ref, y_ref, relayed_ref, out_ref, wide_s, sem):
    _, rows, clips = wide_ref.shape
    index = lax.axis_index("own")
    core = lax.rem(index, CORES)
    chip = lax.div(index, CORES)

    def put(value, flip, core_of):
        at = pl.multiple_of((lax.bitwise_xor(chip, flip) * CORES + core_of) * clips, clips)
        wide_s[:, pl.ds(at, clips)] = value.astype(F32)

    put(wide_ref[0], 0, core)
    put(wide_ref[1], 1, core)
    put(wide_ref[2], 1, 1 - core)
    put(y_ref[core], 2, core)
    put(d_ref[core], 3, core)
    put(relayed_ref[0], 3, 1 - core)
    put(relayed_ref[1], 2, 1 - core)
    put(relayed_ref[2], 0, 1 - core)
    copy = pltpu.make_async_copy(wide_s, out_ref, sem)
    copy.start()
    copy.wait()


def place(*parts):
    rows, clips = parts[0].shape[1:]
    wide = (rows, 8 * clips)
    return pl.pallas_call(
        place_kernel,
        out_shape=jax.ShapeDtypeStruct(wide, F32),
        in_specs=[VMEM] * len(parts),
        out_specs=HBM,
        scratch_shapes=[pltpu.VMEM(wide, F32), pltpu.SemaphoreType.DMA(())],
        compiler_params=pltpu.CompilerParams(vmem_limit_bytes=8 << 20),
    )(*parts)


def per_device_exchanged(planes, queries, block_ids, left_factor, right_factor, clip_grads, lengths):
    size = 4 * CORES

    def move(x, to):
        return lax.ppermute(x, "own", [(i, to(i // CORES, i % CORES)) for i in range(size)])

    def sibling(x):
        return move(x, lambda chip, core: chip * CORES + 1 - core)

    def across(x, flips):
        return move(x, lambda chip, core: (chip ^ flips[core]) * CORES + core)

    flips_a, flips_b = (1, 2), (2, 1)
    row, fac = pack(queries[0], block_ids, left_factor, right_factor)
    slot_d = across(row, (3, 3))
    slot_a = across(row, flips_a)
    factors = [fac]
    held, again = fac, row
    step = 1
    while step < planes:
        got = lax.ppermute(held, "qry", [(i, i ^ step) for i in range(planes)])
        factors.append(got)
        if step * 2 < planes:
            held, again = join(held, got, row)
        step *= 2
    slot_b = across(again, flips_b)
    order_a, order_b = left_factor.shape[2], right_factor.shape[2]
    left_all, right_all = place_factors(factors, order_a, order_b)
    prepared = early(
        [row, sibling(row), slot_d, sibling(slot_d)], left_all, right_all, order_a, order_b
    )
    home, near, x, cross, y, d = score([slot_a, sibling(slot_a), slot_b, sibling(slot_b)], prepared, left_all, right_all, clip_grads, lengths)
    y, d = across(y, (2, 2)), across(d, (3, 3))
    x, cross = across(x, (1, 1)), move(cross, lambda chip, core: (chip ^ 1) * CORES + 1 - core)
    return place(widen(home, x, cross), d, y, sibling(relay(d, y, near)))[None]


def solution(mesh):
    owners, planes = mesh.shape["own"], mesh.shape["qry"]

    def per_device(queries, block_ids, left_factor, right_factor, clip_grads, lengths):
        whole_tiles = left_factor.shape[1] % 16 == 0 and right_factor.shape[1] % 16 == 0
        if owners == 4 * CORES and planes & (planes - 1) == 0 and whole_tiles:
            return per_device_exchanged(
                planes, queries, block_ids, left_factor, right_factor, clip_grads, lengths
            )
        return per_device_gathered(queries, block_ids, left_factor, right_factor, clip_grads, lengths)

    in_specs = (
        P("qry", "own", None),
        P("qry", "own"),
        P(None, "qry", None),
        P(None, "qry", None),
        P("own", None),
        P("own"),
    )
    out_specs = P("qry", "own", None)
    return jax.shard_map(
        per_device, mesh=mesh, in_specs=in_specs, out_specs=out_specs, check_vma=False
    )
```

```python
import jax
import jax.numpy as jnp
from jax import lax
from jax.experimental import pallas as pl
from jax.experimental.pallas import tpu as pltpu
from jax.sharding import PartitionSpec as P

LANES = 128
CORES = 2
HEAD = 256
SOME_VMEM = 16 << 20
VMEM = pl.BlockSpec(memory_space=pltpu.VMEM)
HBM = pl.BlockSpec(memory_space=pltpu.HBM)
F32 = jnp.float32
BF16 = jnp.bfloat16


def precondition(rows, id_values, left_full, right_full):
    blocks = left_full.shape[0]
    order_a = left_full.shape[1]
    order_b = right_full.shape[1]
    labels = jnp.arange(blocks)
    onehot = (id_values[:, :, None] == labels[None, None, :]).astype(F32)
    left_rows = jnp.einsum("srk,kac->srac", onehot, left_full.astype(F32), precision=lax.Precision.HIGHEST)
    right_rows = jnp.einsum("srk,kde->srde", onehot, right_full.astype(F32), precision=lax.Precision.HIGHEST)
    matrix = rows.reshape(rows.shape[0], rows.shape[1], order_a, order_b).astype(F32)
    inner = jnp.einsum("srac,srcd->srad", left_rows, matrix, precision=lax.Precision.HIGHEST)
    outer = jnp.einsum("srad,srde->srae", inner, right_rows, precision=lax.Precision.HIGHEST)
    return outer.reshape(rows.shape).astype(BF16)


def per_device_gathered(queries, block_ids, left_factor, right_factor, clip_grads, lengths):
    left_full = lax.all_gather(left_factor, "qry", axis=1, tiled=True)
    right_full = lax.all_gather(right_factor, "qry", axis=1, tiled=True)
    prepared = precondition(queries, block_ids, left_full, right_full)
    tiles = jnp.einsum(
        "srw,cw->src",
        lax.all_gather(prepared, "own", axis=1, tiled=True),
        clip_grads,
        preferred_element_type=F32,
    )
    factor = lax.rsqrt(F32(queries.shape[2]) * lengths.astype(F32))
    return lax.all_to_all(tiles * factor[None, None, :], "own", split_axis=1, concat_axis=2, tiled=True)


def pack_kernel(q_hbm, ids_hbm, left_hbm, right_hbm, row_ref, fac_ref, ids_s, left_s, sems):
    rows, width = q_hbm.shape
    blocks, cut, order_a = left_s.shape
    copies = [
        pltpu.make_async_copy(ids_hbm, ids_s, sems.at[1]),
        pltpu.make_async_copy(left_hbm, left_s, sems.at[2]),
        pltpu.make_async_copy(right_hbm, fac_ref.at[0, :, cut:, :], sems.at[3]),
    ]
    part = width // 4
    copies = [
        pltpu.make_async_copy(
            q_hbm.at[:, i * part : (i + 1) * part], row_ref.at[:, i * part : (i + 1) * part], sems.at[4 + i]
        )
        for i in range(4)
    ] + copies
    for copy in copies:
        copy.start()
    fac_ref[0, :, :cut, order_a:] = jnp.zeros((blocks, cut, LANES - order_a), BF16)
    square = (rows, rows)
    diagonal = lax.broadcasted_iota(jnp.int32, square, 0) == lax.broadcasted_iota(jnp.int32, square, 1)
    copies[4].wait()
    labels = jnp.where(diagonal, jnp.broadcast_to(ids_s[...].astype(F32), square), 0.0)
    column = jnp.sum(labels, axis=1, keepdims=True)
    column = jnp.broadcast_to(column, (rows, LANES)).astype(BF16)
    row_ref[:, width:] = column
    copies[5].wait()
    fac_ref[0, :, :cut, :order_a] = left_s[...]
    for copy in copies[:4] + copies[6:]:
        copy.wait()


def pack(queries, block_ids, left, right):
    rows, width = queries.shape
    blocks, cut = left.shape[:2]
    depth = cut + right.shape[1]
    return pl.pallas_call(
        pack_kernel,
        out_shape=(
            jax.ShapeDtypeStruct((rows, width + LANES), BF16),
            jax.ShapeDtypeStruct((1, blocks, depth, LANES), BF16),
        ),
        in_specs=[HBM] * 4,
        out_specs=(VMEM, VMEM),
        scratch_shapes=[
            pltpu.VMEM(block_ids.shape, block_ids.dtype),
            pltpu.VMEM(left.shape, left.dtype),
            pltpu.SemaphoreType.DMA((8,)),
        ],
        compiler_params=pltpu.CompilerParams(vmem_limit_bytes=SOME_VMEM),
    )(*(pltpu.with_memory_space_constraint(x, pltpu.HBM) for x in (queries, block_ids, left, right)))


def prepare(slots, left_all, right_all, in_s, mid_s, out_s, prep_ref):
    rows = slots[0].shape[0]
    order_a = left_all.shape[1]
    blocks = left_all.shape[0] // order_a
    order_b = right_all.shape[1] // blocks
    width = order_a * order_b
    pair = 2 * rows

    def label_of(group, n):
        row = slots[2 * group + n // rows][n % rows : n % rows + 1, width:]
        return row.astype(F32)

    for group in range(len(slots) // 2):
        both = slots[2 * group : 2 * group + 2]
        tiles = [
            jnp.concatenate([ref[:, a * order_b : (a + 1) * order_b] for ref in both], axis=0) for a in range(order_a)
        ]
        in_s[group] = jnp.swapaxes(jnp.stack(tiles), 0, 1)
    for group in range(len(slots) // 2):
        for n in range(0, pair, 2):
            x = jnp.concatenate([in_s[group, n + j] for j in range(2)], axis=1)
            inner = jnp.dot(left_all, x, preferred_element_type=F32)
            for j in range(2):
                label = label_of(group, n + j)
                one = inner[:order_a, j * order_b : (j + 1) * order_b]
                for k in range(1, blocks):
                    one = jnp.where(
                        label > k - 0.5,
                        inner[k * order_a : (k + 1) * order_a, j * order_b : (j + 1) * order_b],
                        one,
                    )
                high = one.astype(BF16)
                mid_s[group, n + j, :, :order_b] = high
                mid_s[group, n + j, :, order_b:] = (one - high.astype(F32)).astype(BF16)
    for group in range(len(slots) // 2):
        middle = mid_s[group].reshape(pair * order_a, 2 * order_b)
        outer = jnp.dot(middle, right_all, preferred_element_type=F32)
        for n in range(pair):
            label = label_of(group, n)
            one = outer[n * order_a : (n + 1) * order_a, :order_b]
            for k in range(1, blocks):
                one = jnp.where(
                    label > k - 0.5, outer[n * order_a : (n + 1) * order_a, k * order_b : (k + 1) * order_b], one
                )
            out_s[group, n] = one.astype(BF16)
    for group in range(len(slots) // 2):
        turned = jnp.swapaxes(out_s[group], 0, 1)
        for a in range(order_a):
            prep_ref[group * pair : (group + 1) * pair, a * order_b : (a + 1) * order_b] = turned[a]


def factor_kernel(order_a, order_b, *refs):
    left_ref, right_ref = refs[-2:]
    pieces = [(ref, i) for ref in refs[:-2] for i in range(ref.shape[0])]
    blocks = right_ref.shape[1] // order_b
    cut_a, cut_b = order_a // len(pieces), order_b // len(pieces)
    plane = lax.axis_index("qry")
    for m, (ref, i) in enumerate(pieces):
        piece = ref[i]
        at = lax.bitwise_xor(plane, m)
        for k in range(blocks):
            left_ref[pl.ds(pl.multiple_of(k * order_a + at * cut_a, 16), cut_a), :] = piece[
                :cut_a, k * order_a : (k + 1) * order_a
            ]
            for half in range(2):
                right_ref[
                    pl.ds(pl.multiple_of(half * order_b + at * cut_b, 16), cut_b),
                    k * order_b : (k + 1) * order_b,
                ] = piece[cut_a + k * cut_b : cut_a + (k + 1) * cut_b, :]


def place_factors(factors, blocks, order_a, order_b):
    return pl.pallas_call(
        lambda *refs: factor_kernel(order_a, order_b, *refs),
        out_shape=(
            jax.ShapeDtypeStruct((blocks * order_a, order_a), BF16),
            jax.ShapeDtypeStruct((2 * order_b, blocks * order_b), BF16),
        ),
        in_specs=[VMEM] * len(factors),
        out_specs=(VMEM, VMEM),
        compiler_params=pltpu.CompilerParams(vmem_limit_bytes=8 << 20),
        cost_estimate=pl.CostEstimate(flops=6 * 10**9, bytes_accessed=10**6, transcendentals=0),
    )(*factors)


def early_kernel(nslots, *refs):
    slots = refs[:nslots]
    left_ref, right_ref, prep_ref, in_s, mid_s, out_s = refs[nslots:]
    prepare(slots, left_ref[...], right_ref[...], in_s, mid_s, out_s, prep_ref)


def early(slots, left_all, right_all, order_a, order_b):
    rows = slots[0].shape[0]
    total = len(slots) * rows
    width = order_a * order_b
    return pl.pallas_call(
        lambda *refs: early_kernel(len(slots), *refs),
        out_shape=jax.ShapeDtypeStruct((total, width), BF16),
        in_specs=[VMEM] * (len(slots) + 2),
        out_specs=VMEM,
        scratch_shapes=[
            pltpu.VMEM((len(slots) // 2, 2 * rows, order_a, wide * order_b), BF16) for wide in (1, 2, 1)
        ],
        compiler_params=pltpu.CompilerParams(vmem_limit_bytes=SOME_VMEM),
        cost_estimate=pl.CostEstimate(flops=8 * total * width * order_b, bytes_accessed=4 * total * width, transcendentals=0),
    )(*slots, left_all, right_all)


def score_kernel(nslots, *refs):
    slots = refs[:nslots]
    early_ref, left_ref, right_ref, clips_ref, len_ref = refs[nslots : nslots + 5]
    home_ref, near_ref, x_ref, cross_ref, y_ref, d_ref, in_s, mid_s, out_s, prep_s, all_s = refs[nslots + 5 :]
    width = clips_ref.shape[1]
    rows = slots[0].shape[0]
    prepare(slots, left_ref[...], right_ref[...], in_s, mid_s, out_s, prep_s)
    @pl.when(lax.axis_index("qry") >= 0)
    def _():
        queries = jnp.concatenate([early_ref[...], prep_s[...]], axis=0)
        raw = lax.dot_general(clips_ref[...], queries, (((1,), (1,)), ((), ())), preferred_element_type=F32)
        factor = lax.rsqrt(F32(width) * len_ref[...].astype(F32))
        scores = raw.T * factor
        core = lax.rem(lax.axis_index("own"), CORES)
        for j, (mine, other) in enumerate(((0, 0), (3, 3), (1 + core, 2 - core), (2 - core, 1 + core))):
            at = 2 * j * rows
            all_s[mine, core] = scores[at : at + rows].astype(BF16)
            all_s[other, 1 - core] = scores[at + rows : at + 2 * rows].astype(BF16)
        home_ref[...] = scores[:rows]
        near_ref[...] = all_s[0, 1 - core]
        x_ref[...] = all_s[1, core]
        cross_ref[...] = all_s[1, 1 - core]
        y_ref[...] = all_s[2]
        d_ref[...] = all_s[3]


def score(slots, prepared, left_all, right_all, clip_grads, lengths):
    rows = slots[0].shape[0]
    clips, width = clip_grads.shape
    order_a = left_all.shape[1]
    total = prepared.shape[0] + len(slots) * rows
    return pl.pallas_call(
        lambda *refs: score_kernel(len(slots), *refs),
        out_shape=(
            jax.ShapeDtypeStruct((rows, clips), F32),
            *(jax.ShapeDtypeStruct((rows, clips), BF16),) * 3,
            *(jax.ShapeDtypeStruct((2, rows, clips), BF16),) * 2,
        ),
        in_specs=[VMEM] * (len(slots) + 5),
        out_specs=(VMEM,) * 6,
        scratch_shapes=[
            pltpu.VMEM((len(slots) // 2, 2 * rows, order_a, wide * width // order_a), BF16) for wide in (1, 2, 1)
        ]
        + [pltpu.VMEM((len(slots) * rows, width), BF16), pltpu.VMEM((4, 2, rows, clips), BF16)],
        compiler_params=pltpu.CompilerParams(vmem_limit_bytes=SOME_VMEM),
        cost_estimate=pl.CostEstimate(
            flops=2 * total * width * (clips + 1000), bytes_accessed=clips * width * 2, transcendentals=0
        ),
    )(*slots, prepared, left_all, right_all, clip_grads, lengths.reshape(1, clips))


def in_hbm(x):
    return pltpu.with_memory_space_constraint(x, pltpu.HBM)


def join_kernel(order_a, cut, first_ref, second_ref, row_ref, both_ref, again_ref):
    blocks, depth = first_ref.shape[1:3]
    for j, ref in enumerate((first_ref, second_ref)):
        for k in range(blocks):
            both_ref[j, :cut, k * order_a : (k + 1) * order_a] = ref[0, k, :cut, :order_a]
            at = cut + k * (depth - cut)
            both_ref[j, at : at + depth - cut, :] = ref[0, k, cut:, :]
    again_ref[...] = row_ref[...]


def join(first, second, row, left):
    blocks, cut, order_a = left.shape
    rows = cut + blocks * (first.shape[2] - cut)
    return pl.pallas_call(
        lambda *refs: join_kernel(order_a, cut, *refs),
        out_shape=(
            jax.ShapeDtypeStruct((2, rows, LANES), first.dtype),
            jax.ShapeDtypeStruct(row.shape, row.dtype),
        ),
        in_specs=[VMEM] * 3,
        out_specs=(VMEM, VMEM),
        compiler_params=pltpu.CompilerParams(vmem_limit_bytes=8 << 20),
    )(first, second, row)


def relay_kernel(d_ref, y_ref, near_ref, out_ref):
    other = 1 - lax.rem(lax.axis_index("own"), CORES)
    out_ref[0] = d_ref[other]
    out_ref[1] = y_ref[other]
    out_ref[2] = near_ref[...]


def relay(d, y, near):
    return pl.pallas_call(
        relay_kernel,
        out_shape=jax.ShapeDtypeStruct((3,) + near.shape, near.dtype),
        in_specs=[VMEM] * 3,
        out_specs=VMEM,
        compiler_params=pltpu.CompilerParams(vmem_limit_bytes=8 << 20),
    )(d, y, near)


def widen_kernel(home_ref, x_ref, cross_ref, out_ref):
    for j, ref in enumerate((home_ref, x_ref, cross_ref)):
        out_ref[j] = ref[...].astype(F32)


def widen(*parts):
    return pl.pallas_call(
        widen_kernel,
        out_shape=jax.ShapeDtypeStruct((len(parts),) + parts[0].shape, F32),
        in_specs=[VMEM] * len(parts),
        out_specs=VMEM,
        compiler_params=pltpu.CompilerParams(vmem_limit_bytes=8 << 20),
        cost_estimate=pl.CostEstimate(flops=10**10, bytes_accessed=10**6, transcendentals=0),
    )(*parts)


def place_kernel(wide_ref, d_ref, y_ref, relayed_ref, out_ref, wide_s, sem):
    _, rows, clips = wide_ref.shape
    index = lax.axis_index("own")
    core = lax.rem(index, CORES)
    chip = lax.div(index, CORES)

    def put(value, flip, core_of):
        at = pl.multiple_of((lax.bitwise_xor(chip, flip) * CORES + core_of) * clips, clips)
        wide_s[:, pl.ds(at, clips)] = value.astype(F32)

    put(wide_ref[0], 0, core)
    put(wide_ref[1], 1, core)
    put(wide_ref[2], 1, 1 - core)
    put(y_ref[core], 2, core)
    put(d_ref[core], 3, core)
    put(relayed_ref[0], 3, 1 - core)
    put(relayed_ref[1], 2, 1 - core)
    put(relayed_ref[2], 0, 1 - core)
    copy = pltpu.make_async_copy(wide_s, out_ref, sem)
    copy.start()
    copy.wait()


def place(*parts):
    rows, clips = parts[0].shape[1:]
    wide = (rows, 8 * clips)
    return pl.pallas_call(
        place_kernel,
        out_shape=jax.ShapeDtypeStruct(wide, F32),
        in_specs=[VMEM] * len(parts),
        out_specs=HBM,
        scratch_shapes=[pltpu.VMEM(wide, F32), pltpu.SemaphoreType.DMA(())],
        compiler_params=pltpu.CompilerParams(vmem_limit_bytes=8 << 20),
    )(*parts)


def per_device_exchanged(planes, queries, block_ids, left_factor, right_factor, clip_grads, lengths):
    size = 4 * CORES

    def move(x, to):
        return lax.ppermute(x, "own", [(i, to(i // CORES, i % CORES)) for i in range(size)])

    def sibling(x):
        return move(x, lambda chip, core: chip * CORES + 1 - core)

    def across(x, flips):
        return move(x, lambda chip, core: (chip ^ flips[core]) * CORES + core)

    flips_a, flips_b = (1, 2), (2, 1)
    row, fac = pack(queries[0], block_ids, left_factor, right_factor)
    slot_d = across(row, (3, 3))
    slot_a = across(row, flips_a)
    def plane(x, step):
        return lax.ppermute(x, "qry", [(i, i ^ step) for i in range(planes)])

    held, again = join(fac, plane(fac, 1), row, left_factor)
    factors = [held]
    step = 2
    while step < planes:
        got = plane(held, step)
        factors.append(got)
        if step * 2 < planes:
            held = jnp.concatenate([held, got])
        step *= 2
    slot_b = across(again, flips_b)
    order_a, order_b = left_factor.shape[2], right_factor.shape[2]
    left_all, right_all = place_factors(factors, left_factor.shape[0], order_a, order_b)
    prepared = early(
        [row, sibling(row), slot_d, sibling(slot_d)], left_all, right_all, order_a, order_b
    )
    home, near, x, cross, y, d = score([slot_a, sibling(slot_a), slot_b, sibling(slot_b)], prepared, left_all, right_all, clip_grads, lengths)
    y, d = across(y, (2, 2)), across(d, (3, 3))
    x, cross = across(x, (1, 1)), move(cross, lambda chip, core: (chip ^ 1) * CORES + 1 - core)
    return place(widen(home, x, cross), d, y, sibling(relay(d, y, near)))[None]


def solution(mesh):
    owners, planes = mesh.shape["own"], mesh.shape["qry"]

    def per_device(queries, block_ids, left_factor, right_factor, clip_grads, lengths):
        whole_tiles = left_factor.shape[1] % 16 == 0 and right_factor.shape[1] % 16 == 0
        whole_tiles = whole_tiles and left_factor.shape[0] * left_factor.shape[2] == LANES == right_factor.shape[2]
        if owners == 4 * CORES and planes > 1 and planes & (planes - 1) == 0 and whole_tiles:
            return per_device_exchanged(
                planes, queries, block_ids, left_factor, right_factor, clip_grads, lengths
            )
        return per_device_gathered(queries, block_ids, left_factor, right_factor, clip_grads, lengths)

    in_specs = (
        P("qry", "own", None),
        P("qry", "own"),
        P(None, "qry", None),
        P(None, "qry", None),
        P("own", None),
        P("own"),
    )
    out_specs = P("qry", "own", None)
    return jax.shard_map(
        per_device, mesh=mesh, in_specs=in_specs, out_specs=out_specs, check_vma=False
    )
```

```python
import jax
import jax.numpy as jnp
from jax import lax
from jax.experimental import pallas as pl
from jax.experimental.pallas import tpu as pltpu
from jax.sharding import PartitionSpec as P

LANES = 128
CORES = 2
SOME_VMEM = 16 << 20
SMALL_VMEM = 8 << 20
FACTORS_FIRST = 6 * 10**9
STRAIGHT_FIRST = 10**10
VMEM = pl.BlockSpec(memory_space=pltpu.VMEM)
HBM = pl.BlockSpec(memory_space=pltpu.HBM)
F32 = jnp.float32
BF16 = jnp.bfloat16


def precondition(rows, id_values, left_full, right_full):
    blocks = left_full.shape[0]
    order_a = left_full.shape[1]
    order_b = right_full.shape[1]
    labels = jnp.arange(blocks)
    onehot = (id_values[:, :, None] == labels[None, None, :]).astype(F32)
    left_rows = jnp.einsum("srk,kac->srac", onehot, left_full.astype(F32), precision=lax.Precision.HIGHEST)
    right_rows = jnp.einsum("srk,kde->srde", onehot, right_full.astype(F32), precision=lax.Precision.HIGHEST)
    matrix = rows.reshape(rows.shape[0], rows.shape[1], order_a, order_b).astype(F32)
    inner = jnp.einsum("srac,srcd->srad", left_rows, matrix, precision=lax.Precision.HIGHEST)
    outer = jnp.einsum("srad,srde->srae", inner, right_rows, precision=lax.Precision.HIGHEST)
    return outer.reshape(rows.shape).astype(BF16)


def per_device_gathered(queries, block_ids, left_factor, right_factor, clip_grads, lengths):
    left_full = lax.all_gather(left_factor, "qry", axis=1, tiled=True)
    right_full = lax.all_gather(right_factor, "qry", axis=1, tiled=True)
    prepared = precondition(queries, block_ids, left_full, right_full)
    tiles = jnp.einsum(
        "srw,cw->src",
        lax.all_gather(prepared, "own", axis=1, tiled=True),
        clip_grads,
        preferred_element_type=F32,
    )
    factor = lax.rsqrt(F32(queries.shape[2]) * lengths.astype(F32))
    return lax.all_to_all(tiles * factor[None, None, :], "own", split_axis=1, concat_axis=2, tiled=True)


def pack_kernel(q_hbm, ids_hbm, left_hbm, right_hbm, row_ref, fac_ref, ids_s, left_s, sems):
    rows, width = q_hbm.shape
    blocks, cut, order_a = left_s.shape
    copies = [
        pltpu.make_async_copy(ids_hbm, ids_s, sems.at[1]),
        pltpu.make_async_copy(left_hbm, left_s, sems.at[2]),
        pltpu.make_async_copy(right_hbm, fac_ref.at[0, :, cut:, :], sems.at[3]),
    ]
    part = width // 4
    copies = [
        pltpu.make_async_copy(
            q_hbm.at[:, i * part : (i + 1) * part], row_ref.at[:, i * part : (i + 1) * part], sems.at[4 + i]
        )
        for i in range(4)
    ] + copies
    for copy in copies:
        copy.start()
    fac_ref[0, :, :cut, order_a:] = jnp.zeros((blocks, cut, LANES - order_a), BF16)
    square = (rows, rows)
    diagonal = lax.broadcasted_iota(jnp.int32, square, 0) == lax.broadcasted_iota(jnp.int32, square, 1)
    copies[4].wait()
    labels = jnp.where(diagonal, jnp.broadcast_to(ids_s[...].astype(F32), square), 0.0)
    column = jnp.sum(labels, axis=1, keepdims=True)
    column = jnp.broadcast_to(column, (rows, LANES)).astype(BF16)
    row_ref[:, width:] = column
    copies[5].wait()
    fac_ref[0, :, :cut, :order_a] = left_s[...]
    for copy in copies[:4] + copies[6:]:
        copy.wait()


def in_hbm(x):
    return pltpu.with_memory_space_constraint(x, pltpu.HBM)


def pack(queries, block_ids, left, right):
    rows, width = queries.shape
    blocks, cut = left.shape[:2]
    depth = cut + right.shape[1]
    return pl.pallas_call(
        pack_kernel,
        out_shape=(
            jax.ShapeDtypeStruct((rows, width + LANES), BF16),
            jax.ShapeDtypeStruct((1, blocks, depth, LANES), BF16),
        ),
        in_specs=[HBM] * 4,
        out_specs=(VMEM, VMEM),
        scratch_shapes=[
            pltpu.VMEM(block_ids.shape, block_ids.dtype),
            pltpu.VMEM(left.shape, left.dtype),
            pltpu.SemaphoreType.DMA((8,)),
        ],
        compiler_params=pltpu.CompilerParams(vmem_limit_bytes=SOME_VMEM),
    )(*(in_hbm(x) for x in (queries, block_ids, left, right)))


def prepare(slots, left_all, right_all, in_s, mid_s, out_s, prep_ref):
    rows = slots[0].shape[0]
    order_a = left_all.shape[1]
    blocks = left_all.shape[0] // order_a
    order_b = right_all.shape[1] // blocks
    width = order_a * order_b
    pair = 2 * rows

    def label_of(group, n):
        row = slots[2 * group + n // rows][n % rows : n % rows + 1, width:]
        return row.astype(F32)

    for group in range(len(slots) // 2):
        both = slots[2 * group : 2 * group + 2]
        tiles = [
            jnp.concatenate([ref[:, a * order_b : (a + 1) * order_b] for ref in both], axis=0) for a in range(order_a)
        ]
        in_s[group] = jnp.swapaxes(jnp.stack(tiles), 0, 1)
    for group in range(len(slots) // 2):
        for n in range(0, pair, 2):
            x = jnp.concatenate([in_s[group, n + j] for j in range(2)], axis=1)
            inner = jnp.dot(left_all, x, preferred_element_type=F32)
            for j in range(2):
                label = label_of(group, n + j)
                one = inner[:order_a, j * order_b : (j + 1) * order_b]
                for k in range(1, blocks):
                    one = jnp.where(
                        label > k - 0.5,
                        inner[k * order_a : (k + 1) * order_a, j * order_b : (j + 1) * order_b],
                        one,
                    )
                high = one.astype(BF16)
                mid_s[group, n + j, :, :order_b] = high
                mid_s[group, n + j, :, order_b:] = (one - high.astype(F32)).astype(BF16)
    for group in range(len(slots) // 2):
        middle = mid_s[group].reshape(pair * order_a, 2 * order_b)
        outer = jnp.dot(middle, right_all, preferred_element_type=F32)
        for n in range(pair):
            label = label_of(group, n)
            one = outer[n * order_a : (n + 1) * order_a, :order_b]
            for k in range(1, blocks):
                one = jnp.where(
                    label > k - 0.5, outer[n * order_a : (n + 1) * order_a, k * order_b : (k + 1) * order_b], one
                )
            out_s[group, n] = one.astype(BF16)
    for group in range(len(slots) // 2):
        turned = jnp.swapaxes(out_s[group], 0, 1)
        for a in range(order_a):
            prep_ref[group * pair : (group + 1) * pair, a * order_b : (a + 1) * order_b] = turned[a]


def factor_kernel(order_a, order_b, *refs):
    left_ref, right_ref = refs[-2:]
    pieces = [(ref, i) for ref in refs[:-2] for i in range(ref.shape[0])]
    blocks = right_ref.shape[1] // order_b
    cut_a, cut_b = order_a // len(pieces), order_b // len(pieces)
    plane = lax.axis_index("qry")
    for m, (ref, i) in enumerate(pieces):
        piece = ref[i]
        at = lax.bitwise_xor(plane, m)
        for k in range(blocks):
            left_ref[pl.ds(pl.multiple_of(k * order_a + at * cut_a, 16), cut_a), :] = piece[
                :cut_a, k * order_a : (k + 1) * order_a
            ]
            for half in range(2):
                right_ref[
                    pl.ds(pl.multiple_of(half * order_b + at * cut_b, 16), cut_b),
                    k * order_b : (k + 1) * order_b,
                ] = piece[cut_a + k * cut_b : cut_a + (k + 1) * cut_b, :]


def place_factors(factors, blocks, order_a, order_b):
    return pl.pallas_call(
        lambda *refs: factor_kernel(order_a, order_b, *refs),
        out_shape=(
            jax.ShapeDtypeStruct((blocks * order_a, order_a), BF16),
            jax.ShapeDtypeStruct((2 * order_b, blocks * order_b), BF16),
        ),
        in_specs=[VMEM] * len(factors),
        out_specs=(VMEM, VMEM),
        compiler_params=pltpu.CompilerParams(vmem_limit_bytes=SMALL_VMEM),
        cost_estimate=pl.CostEstimate(flops=FACTORS_FIRST, bytes_accessed=10**6, transcendentals=0),
    )(*factors)


def early_kernel(nslots, *refs):
    slots = refs[:nslots]
    left_ref, right_ref, prep_ref, in_s, mid_s, out_s = refs[nslots:]
    prepare(slots, left_ref[...], right_ref[...], in_s, mid_s, out_s, prep_ref)


def early(slots, left_all, right_all, order_a, order_b):
    rows = slots[0].shape[0]
    total = len(slots) * rows
    width = order_a * order_b
    return pl.pallas_call(
        lambda *refs: early_kernel(len(slots), *refs),
        out_shape=jax.ShapeDtypeStruct((total, width), BF16),
        in_specs=[VMEM] * (len(slots) + 2),
        out_specs=VMEM,
        scratch_shapes=[
            pltpu.VMEM((len(slots) // 2, 2 * rows, order_a, wide * order_b), BF16) for wide in (1, 2, 1)
        ],
        compiler_params=pltpu.CompilerParams(vmem_limit_bytes=SOME_VMEM),
        cost_estimate=pl.CostEstimate(flops=8 * total * width * order_b, bytes_accessed=4 * total * width, transcendentals=0),
    )(*slots, left_all, right_all)


def score_kernel(nslots, *refs):
    slots = refs[:nslots]
    early_ref, left_ref, right_ref, clips_ref, len_ref = refs[nslots : nslots + 5]
    home_ref, near_ref, x_ref, cross_ref, y_ref, d_ref, in_s, mid_s, out_s, prep_s, all_s = refs[nslots + 5 :]
    width = clips_ref.shape[1]
    rows = slots[0].shape[0]
    prepare(slots, left_ref[...], right_ref[...], in_s, mid_s, out_s, prep_s)

    @pl.when(lax.axis_index("qry") >= 0)
    def _():
        queries = jnp.concatenate([early_ref[...], prep_s[...]], axis=0)
        raw = lax.dot_general(clips_ref[...], queries, (((1,), (1,)), ((), ())), preferred_element_type=F32)
        factor = lax.rsqrt(F32(width) * len_ref[...].astype(F32))
        scores = raw.T * factor
        core = lax.rem(lax.axis_index("own"), CORES)
        for j, (mine, other) in enumerate(((0, 0), (3, 3), (1 + core, 2 - core), (2 - core, 1 + core))):
            at = j * rows
            all_s[mine, core] = scores[at : at + rows].astype(BF16)
            at += scores.shape[0] // 2
            all_s[other, 1 - core] = scores[at : at + rows].astype(BF16)
        home_ref[...] = scores[:rows]
        near_ref[...] = all_s[0, 1 - core]
        x_ref[...] = all_s[1, core]
        cross_ref[...] = all_s[1, 1 - core]
        y_ref[...] = all_s[2]
        d_ref[...] = all_s[3]


def score(slots, prepared, left_all, right_all, clip_grads, lengths):
    rows = slots[0].shape[0]
    clips, width = clip_grads.shape
    order_a = left_all.shape[1]
    total = prepared.shape[0] + len(slots) * rows
    return pl.pallas_call(
        lambda *refs: score_kernel(len(slots), *refs),
        out_shape=(
            jax.ShapeDtypeStruct((rows, clips), F32),
            *(jax.ShapeDtypeStruct((rows, clips), BF16),) * 3,
            *(jax.ShapeDtypeStruct((2, rows, clips), BF16),) * 2,
        ),
        in_specs=[VMEM] * (len(slots) + 5),
        out_specs=(VMEM,) * 6,
        scratch_shapes=[
            pltpu.VMEM((len(slots) // 2, 2 * rows, order_a, wide * width // order_a), BF16) for wide in (1, 2, 1)
        ]
        + [pltpu.VMEM((len(slots) * rows, width), BF16), pltpu.VMEM((4, 2, rows, clips), BF16)],
        compiler_params=pltpu.CompilerParams(vmem_limit_bytes=SOME_VMEM),
        cost_estimate=pl.CostEstimate(
            flops=2 * total * width * (clips + 1000), bytes_accessed=clips * width * 2, transcendentals=0
        ),
    )(*slots, prepared, left_all, right_all, clip_grads, lengths.reshape(1, clips))


def join_kernel(order_a, cut, first_ref, second_ref, row_ref, both_ref, again_ref):
    blocks, depth = first_ref.shape[1:3]
    for j, ref in enumerate((first_ref, second_ref)):
        for k in range(blocks):
            both_ref[j, :cut, k * order_a : (k + 1) * order_a] = ref[0, k, :cut, :order_a]
            at = cut + k * (depth - cut)
            both_ref[j, at : at + depth - cut, :] = ref[0, k, cut:, :]
    again_ref[...] = row_ref[...]


def join(first, second, row, left):
    blocks, cut, order_a = left.shape
    rows = cut + blocks * (first.shape[2] - cut)
    return pl.pallas_call(
        lambda *refs: join_kernel(order_a, cut, *refs),
        out_shape=(
            jax.ShapeDtypeStruct((2, rows, LANES), first.dtype),
            jax.ShapeDtypeStruct(row.shape, row.dtype),
        ),
        in_specs=[VMEM] * 3,
        out_specs=(VMEM, VMEM),
        compiler_params=pltpu.CompilerParams(vmem_limit_bytes=SMALL_VMEM),
    )(first, second, row)


def relay_kernel(d_ref, y_ref, near_ref, out_ref):
    other = 1 - lax.rem(lax.axis_index("own"), CORES)
    out_ref[0] = d_ref[other]
    out_ref[1] = y_ref[other]
    out_ref[2] = near_ref[...]


def relay(d, y, near):
    return pl.pallas_call(
        relay_kernel,
        out_shape=jax.ShapeDtypeStruct((3,) + near.shape, near.dtype),
        in_specs=[VMEM] * 3,
        out_specs=VMEM,
        compiler_params=pltpu.CompilerParams(vmem_limit_bytes=SMALL_VMEM),
    )(d, y, near)


def widen_kernel(home_ref, x_ref, cross_ref, out_ref):
    for j, ref in enumerate((home_ref, x_ref, cross_ref)):
        out_ref[j] = ref[...].astype(F32)


def widen(*parts):
    return pl.pallas_call(
        widen_kernel,
        out_shape=jax.ShapeDtypeStruct((len(parts),) + parts[0].shape, F32),
        in_specs=[VMEM] * len(parts),
        out_specs=VMEM,
        compiler_params=pltpu.CompilerParams(vmem_limit_bytes=SMALL_VMEM),
        cost_estimate=pl.CostEstimate(flops=STRAIGHT_FIRST, bytes_accessed=10**6, transcendentals=0),
    )(*parts)


def place_kernel(wide_ref, d_ref, y_ref, relayed_ref, out_ref, wide_s, sem):
    _, rows, clips = wide_ref.shape
    index = lax.axis_index("own")
    core = lax.rem(index, CORES)
    chip = lax.div(index, CORES)

    def put(value, flip, core_of):
        at = pl.multiple_of((lax.bitwise_xor(chip, flip) * CORES + core_of) * clips, clips)
        wide_s[:, pl.ds(at, clips)] = value.astype(F32)

    put(wide_ref[0], 0, core)
    put(wide_ref[1], 1, core)
    put(wide_ref[2], 1, 1 - core)
    put(y_ref[core], 2, core)
    put(d_ref[core], 3, core)
    put(relayed_ref[0], 3, 1 - core)
    put(relayed_ref[1], 2, 1 - core)
    put(relayed_ref[2], 0, 1 - core)
    copy = pltpu.make_async_copy(wide_s, out_ref, sem)
    copy.start()
    copy.wait()


def place(*parts):
    rows, clips = parts[0].shape[1:]
    wide = (rows, 8 * clips)
    return pl.pallas_call(
        place_kernel,
        out_shape=jax.ShapeDtypeStruct(wide, F32),
        in_specs=[VMEM] * len(parts),
        out_specs=HBM,
        scratch_shapes=[pltpu.VMEM(wide, F32), pltpu.SemaphoreType.DMA(())],
        compiler_params=pltpu.CompilerParams(vmem_limit_bytes=SMALL_VMEM),
    )(*parts)


def per_device_exchanged(planes, queries, block_ids, left_factor, right_factor, clip_grads, lengths):
    size = 4 * CORES

    def move(x, to):
        return lax.ppermute(x, "own", [(i, to(i // CORES, i % CORES)) for i in range(size)])

    def sibling(x):
        return move(x, lambda chip, core: chip * CORES + 1 - core)

    def across(x, flips):
        return move(x, lambda chip, core: (chip ^ flips[core]) * CORES + core)

    def plane(x, step):
        return lax.ppermute(x, "qry", [(i, i ^ step) for i in range(planes)])

    flips_a, flips_b = (1, 2), (2, 1)
    row, fac = pack(queries[0], block_ids, left_factor, right_factor)
    slot_d = across(row, (3, 3))
    slot_a = across(row, flips_a)
    held, again = join(fac, plane(fac, 1), row, left_factor)
    factors = [held]
    step = 2
    while step < planes:
        got = plane(held, step)
        factors.append(got)
        if step * 2 < planes:
            held = jnp.concatenate([held, got])
        step *= 2
    slot_b = across(again, flips_b)
    order_a, order_b = left_factor.shape[2], right_factor.shape[2]
    left_all, right_all = place_factors(factors, left_factor.shape[0], order_a, order_b)
    prepared = early([row, slot_d, slot_a, slot_b], left_all, right_all, order_a, order_b)
    passed = [sibling(row), sibling(slot_d), sibling(slot_a), sibling(slot_b)]
    home, near, x, cross, y, d = score(passed, prepared, left_all, right_all, clip_grads, lengths)
    y, d = across(y, (2, 2)), across(d, (3, 3))
    x, cross = across(x, (1, 1)), move(cross, lambda chip, core: (chip ^ 1) * CORES + 1 - core)
    return place(widen(home, x, cross), d, y, sibling(relay(d, y, near)))[None]


def solution(mesh):
    owners, planes = mesh.shape["own"], mesh.shape["qry"]

    def per_device(queries, block_ids, left_factor, right_factor, clip_grads, lengths):
        whole_tiles = left_factor.shape[1] % 16 == 0 and right_factor.shape[1] % 16 == 0
        whole_tiles = whole_tiles and left_factor.shape[0] * left_factor.shape[2] == LANES == right_factor.shape[2]
        if owners == 4 * CORES and planes > 1 and planes & (planes - 1) == 0 and whole_tiles:
            return per_device_exchanged(
                planes, queries, block_ids, left_factor, right_factor, clip_grads, lengths
            )
        return per_device_gathered(queries, block_ids, left_factor, right_factor, clip_grads, lengths)

    in_specs = (
        P("qry", "own", None),
        P("qry", "own"),
        P(None, "qry", None),
        P(None, "qry", None),
        P("own", None),
        P("own"),
    )
    out_specs = P("qry", "own", None)
    return jax.shard_map(
        per_device, mesh=mesh, in_specs=in_specs, out_specs=out_specs, check_vma=False
    )
```

```python
import jax
import jax.numpy as jnp
from jax import lax
from jax.experimental import pallas as pl
from jax.experimental.pallas import tpu as pltpu
from jax.sharding import PartitionSpec as P

LANES = 128
CORES = 2
SIDE = 8
SOME_VMEM = 16 << 20
SMALL_VMEM = 8 << 20
FACTORS_FIRST = 6 * 10**9
STRAIGHT_FIRST = 10**10
VMEM = pl.BlockSpec(memory_space=pltpu.VMEM)
HBM = pl.BlockSpec(memory_space=pltpu.HBM)
F32 = jnp.float32
BF16 = jnp.bfloat16


def precondition(rows, id_values, left_full, right_full):
    blocks = left_full.shape[0]
    order_a = left_full.shape[1]
    order_b = right_full.shape[1]
    labels = jnp.arange(blocks)
    onehot = (id_values[:, :, None] == labels[None, None, :]).astype(F32)
    left_rows = jnp.einsum("srk,kac->srac", onehot, left_full.astype(F32), precision=lax.Precision.HIGHEST)
    right_rows = jnp.einsum("srk,kde->srde", onehot, right_full.astype(F32), precision=lax.Precision.HIGHEST)
    matrix = rows.reshape(rows.shape[0], rows.shape[1], order_a, order_b).astype(F32)
    inner = jnp.einsum("srac,srcd->srad", left_rows, matrix, precision=lax.Precision.HIGHEST)
    outer = jnp.einsum("srad,srde->srae", inner, right_rows, precision=lax.Precision.HIGHEST)
    return outer.reshape(rows.shape).astype(BF16)


def per_device_gathered(queries, block_ids, left_factor, right_factor, clip_grads, lengths):
    left_full = lax.all_gather(left_factor, "qry", axis=1, tiled=True)
    right_full = lax.all_gather(right_factor, "qry", axis=1, tiled=True)
    prepared = precondition(queries, block_ids, left_full, right_full)
    tiles = jnp.einsum(
        "srw,cw->src",
        lax.all_gather(prepared, "own", axis=1, tiled=True),
        clip_grads,
        preferred_element_type=F32,
    )
    factor = lax.rsqrt(F32(queries.shape[2]) * lengths.astype(F32))
    return lax.all_to_all(tiles * factor[None, None, :], "own", split_axis=1, concat_axis=2, tiled=True)


def pack_kernel(q_hbm, ids_hbm, left_hbm, right_hbm, row_ref, fac_ref, ids_s, left_s, sems):
    rows, width = q_hbm.shape
    blocks, cut, order_a = left_s.shape
    copies = [
        pltpu.make_async_copy(ids_hbm, ids_s, sems.at[1]),
        pltpu.make_async_copy(left_hbm, left_s, sems.at[2]),
        pltpu.make_async_copy(right_hbm, fac_ref.at[0, :, cut:, :], sems.at[3]),
    ]
    part = width // 4
    copies = [
        pltpu.make_async_copy(
            q_hbm.at[:, i * part : (i + 1) * part], row_ref.at[:, i * part : (i + 1) * part], sems.at[4 + i]
        )
        for i in range(4)
    ] + copies
    for copy in copies:
        copy.start()
    fac_ref[0, :, :cut, order_a:] = jnp.zeros((blocks, cut, LANES - order_a), BF16)
    square = (rows, rows)
    diagonal = lax.broadcasted_iota(jnp.int32, square, 0) == lax.broadcasted_iota(jnp.int32, square, 1)
    copies[4].wait()
    labels = jnp.where(diagonal, jnp.broadcast_to(ids_s[...].astype(F32), square), 0.0)
    column = jnp.sum(labels, axis=1, keepdims=True)
    column = jnp.broadcast_to(column, (rows, LANES)).astype(BF16)
    row_ref[:, width:] = column
    copies[5].wait()
    fac_ref[0, :, :cut, :order_a] = left_s[...]
    for copy in copies[:4] + copies[6:]:
        copy.wait()


def in_hbm(x):
    return pltpu.with_memory_space_constraint(x, pltpu.HBM)


def pack(queries, block_ids, left, right):
    rows, width = queries.shape
    blocks, cut = left.shape[:2]
    depth = cut + right.shape[1]
    return pl.pallas_call(
        pack_kernel,
        out_shape=(
            jax.ShapeDtypeStruct((rows, width + LANES), BF16),
            jax.ShapeDtypeStruct((1, blocks, depth, LANES), BF16),
        ),
        in_specs=[HBM] * 4,
        out_specs=(VMEM, VMEM),
        scratch_shapes=[
            pltpu.VMEM(block_ids.shape, block_ids.dtype),
            pltpu.VMEM(left.shape, left.dtype),
            pltpu.SemaphoreType.DMA((8,)),
        ],
        compiler_params=pltpu.CompilerParams(vmem_limit_bytes=SOME_VMEM),
    )(*(in_hbm(x) for x in (queries, block_ids, left, right)))


def prepare(slots, left_all, right_all, in_s, mid_s, out_s, prep_ref):
    rows = slots[0].shape[0]
    order_a = left_all.shape[1]
    blocks = left_all.shape[0] // order_a
    order_b = right_all.shape[1] // blocks
    width = order_a * order_b
    pair = 2 * rows

    def label_of(group, n):
        row = slots[2 * group + n // rows][n % rows : n % rows + 1, width:]
        return row.astype(F32)

    for group in range(len(slots) // 2):
        both = slots[2 * group : 2 * group + 2]
        tiles = [
            jnp.concatenate([ref[:, a * order_b : (a + 1) * order_b] for ref in both], axis=0) for a in range(order_a)
        ]
        in_s[group] = jnp.swapaxes(jnp.stack(tiles), 0, 1)
    for group in range(len(slots) // 2):
        for n in range(0, pair, 2):
            x = jnp.concatenate([in_s[group, n + j] for j in range(2)], axis=1)
            inner = jnp.dot(left_all, x, preferred_element_type=F32)
            for j in range(2):
                label = label_of(group, n + j)
                one = inner[:order_a, j * order_b : (j + 1) * order_b]
                for k in range(1, blocks):
                    one = jnp.where(
                        label > k - 0.5,
                        inner[k * order_a : (k + 1) * order_a, j * order_b : (j + 1) * order_b],
                        one,
                    )
                high = one.astype(BF16)
                mid_s[group, n + j, :, :order_b] = high
                mid_s[group, n + j, :, order_b:] = (one - high.astype(F32)).astype(BF16)
    for group in range(len(slots) // 2):
        for first in range(0, pair, SIDE):
            middle = mid_s[group, first : first + SIDE].reshape(SIDE * order_a, 2 * order_b)
            outer = jnp.dot(middle, right_all, preferred_element_type=F32)
            for j in range(SIDE):
                label = label_of(group, first + j)
                one = outer[j * order_a : (j + 1) * order_a, :order_b]
                for k in range(1, blocks):
                    one = jnp.where(
                        label > k - 0.5,
                        outer[j * order_a : (j + 1) * order_a, k * order_b : (k + 1) * order_b],
                        one,
                    )
                out_s[group, first + j] = one.astype(BF16)
    for group in range(len(slots) // 2):
        turned = jnp.swapaxes(out_s[group], 0, 1)
        for a in range(order_a):
            prep_ref[group * pair : (group + 1) * pair, a * order_b : (a + 1) * order_b] = turned[a]


def factor_kernel(order_a, order_b, *refs):
    left_ref, right_ref = refs[-2:]
    pieces = [(ref, i) for ref in refs[:-2] for i in range(ref.shape[0])]
    blocks = right_ref.shape[1] // order_b
    cut_a, cut_b = order_a // len(pieces), order_b // len(pieces)
    plane = lax.axis_index("qry")
    for m, (ref, i) in enumerate(pieces):
        piece = ref[i]
        at = lax.bitwise_xor(plane, m)
        for k in range(blocks):
            left_ref[pl.ds(pl.multiple_of(k * order_a + at * cut_a, 16), cut_a), :] = piece[
                :cut_a, k * order_a : (k + 1) * order_a
            ]
            for half in range(2):
                right_ref[
                    pl.ds(pl.multiple_of(half * order_b + at * cut_b, 16), cut_b),
                    k * order_b : (k + 1) * order_b,
                ] = piece[cut_a + k * cut_b : cut_a + (k + 1) * cut_b, :]


def place_factors(factors, blocks, order_a, order_b):
    return pl.pallas_call(
        lambda *refs: factor_kernel(order_a, order_b, *refs),
        out_shape=(
            jax.ShapeDtypeStruct((blocks * order_a, order_a), BF16),
            jax.ShapeDtypeStruct((2 * order_b, blocks * order_b), BF16),
        ),
        in_specs=[VMEM] * len(factors),
        out_specs=(VMEM, VMEM),
        compiler_params=pltpu.CompilerParams(vmem_limit_bytes=SMALL_VMEM),
        cost_estimate=pl.CostEstimate(flops=FACTORS_FIRST, bytes_accessed=10**6, transcendentals=0),
    )(*factors)


def early_kernel(nslots, *refs):
    slots = refs[:nslots]
    left_ref, right_ref, prep_ref, in_s, mid_s, out_s = refs[nslots:]
    prepare(slots, left_ref[...], right_ref[...], in_s, mid_s, out_s, prep_ref)


def early(slots, left_all, right_all, order_a, order_b):
    rows = slots[0].shape[0]
    total = len(slots) * rows
    width = order_a * order_b
    return pl.pallas_call(
        lambda *refs: early_kernel(len(slots), *refs),
        out_shape=jax.ShapeDtypeStruct((total, width), BF16),
        in_specs=[VMEM] * (len(slots) + 2),
        out_specs=VMEM,
        scratch_shapes=[
            pltpu.VMEM((len(slots) // 2, 2 * rows, order_a, wide * order_b), BF16) for wide in (1, 2, 1)
        ],
        compiler_params=pltpu.CompilerParams(vmem_limit_bytes=SOME_VMEM),
        cost_estimate=pl.CostEstimate(flops=8 * total * width * order_b, bytes_accessed=4 * total * width, transcendentals=0),
    )(*slots, left_all, right_all)


def score_kernel(nslots, *refs):
    slots = refs[:nslots]
    early_ref, left_ref, right_ref, clips_ref, len_ref = refs[nslots : nslots + 5]
    home_ref, near_ref, x_ref, cross_ref, y_ref, d_ref, in_s, mid_s, out_s, prep_s, all_s = refs[nslots + 5 :]
    width = clips_ref.shape[1]
    rows = slots[0].shape[0]
    prepare(slots, left_ref[...], right_ref[...], in_s, mid_s, out_s, prep_s)

    @pl.when(lax.axis_index("qry") >= 0)
    def _():
        queries = jnp.concatenate([early_ref[...], prep_s[...]], axis=0)
        raw = lax.dot_general(clips_ref[...], queries, (((1,), (1,)), ((), ())), preferred_element_type=F32)
        factor = lax.rsqrt(F32(width) * len_ref[...].astype(F32))
        scores = raw.T * factor
        core = lax.rem(lax.axis_index("own"), CORES)
        for j, (mine, other) in enumerate(((0, 0), (3, 3), (1 + core, 2 - core), (2 - core, 1 + core))):
            at = j * rows
            all_s[mine, core] = scores[at : at + rows].astype(BF16)
            at += scores.shape[0] // 2
            all_s[other, 1 - core] = scores[at : at + rows].astype(BF16)
        home_ref[...] = scores[:rows]
        near_ref[...] = all_s[0, 1 - core]
        x_ref[...] = all_s[1, core]
        cross_ref[...] = all_s[1, 1 - core]
        y_ref[...] = all_s[2]
        d_ref[...] = all_s[3]


def score(slots, prepared, left_all, right_all, clip_grads, lengths):
    rows = slots[0].shape[0]
    clips, width = clip_grads.shape
    order_a = left_all.shape[1]
    total = prepared.shape[0] + len(slots) * rows
    return pl.pallas_call(
        lambda *refs: score_kernel(len(slots), *refs),
        out_shape=(
            jax.ShapeDtypeStruct((rows, clips), F32),
            *(jax.ShapeDtypeStruct((rows, clips), BF16),) * 3,
            *(jax.ShapeDtypeStruct((2, rows, clips), BF16),) * 2,
        ),
        in_specs=[VMEM] * (len(slots) + 5),
        out_specs=(VMEM,) * 6,
        scratch_shapes=[
            pltpu.VMEM((len(slots) // 2, 2 * rows, order_a, wide * width // order_a), BF16) for wide in (1, 2, 1)
        ]
        + [pltpu.VMEM((len(slots) * rows, width), BF16), pltpu.VMEM((4, 2, rows, clips), BF16)],
        compiler_params=pltpu.CompilerParams(vmem_limit_bytes=SOME_VMEM),
        cost_estimate=pl.CostEstimate(
            flops=2 * total * width * (clips + 1000), bytes_accessed=clips * width * 2, transcendentals=0
        ),
    )(*slots, prepared, left_all, right_all, clip_grads, lengths.reshape(1, clips))


def join_kernel(order_a, cut, first_ref, second_ref, row_ref, both_ref, again_ref):
    blocks, depth = first_ref.shape[1:3]
    for j, ref in enumerate((first_ref, second_ref)):
        for k in range(blocks):
            both_ref[j, :cut, k * order_a : (k + 1) * order_a] = ref[0, k, :cut, :order_a]
            at = cut + k * (depth - cut)
            both_ref[j, at : at + depth - cut, :] = ref[0, k, cut:, :]
    again_ref[...] = row_ref[...]


def join(first, second, row, left):
    blocks, cut, order_a = left.shape
    rows = cut + blocks * (first.shape[2] - cut)
    return pl.pallas_call(
        lambda *refs: join_kernel(order_a, cut, *refs),
        out_shape=(
            jax.ShapeDtypeStruct((2, rows, LANES), first.dtype),
            jax.ShapeDtypeStruct(row.shape, row.dtype),
        ),
        in_specs=[VMEM] * 3,
        out_specs=(VMEM, VMEM),
        compiler_params=pltpu.CompilerParams(vmem_limit_bytes=SMALL_VMEM),
    )(first, second, row)


def relay_kernel(d_ref, y_ref, near_ref, out_ref):
    other = 1 - lax.rem(lax.axis_index("own"), CORES)
    out_ref[0] = d_ref[other]
    out_ref[1] = y_ref[other]
    out_ref[2] = near_ref[...]


def relay(d, y, near):
    return pl.pallas_call(
        relay_kernel,
        out_shape=jax.ShapeDtypeStruct((3,) + near.shape, near.dtype),
        in_specs=[VMEM] * 3,
        out_specs=VMEM,
        compiler_params=pltpu.CompilerParams(vmem_limit_bytes=SMALL_VMEM),
    )(d, y, near)


def widen_kernel(home_ref, x_ref, cross_ref, out_ref):
    for j, ref in enumerate((home_ref, x_ref, cross_ref)):
        out_ref[j] = ref[...].astype(F32)


def widen(*parts):
    return pl.pallas_call(
        widen_kernel,
        out_shape=jax.ShapeDtypeStruct((len(parts),) + parts[0].shape, F32),
        in_specs=[VMEM] * len(parts),
        out_specs=VMEM,
        compiler_params=pltpu.CompilerParams(vmem_limit_bytes=SMALL_VMEM),
        cost_estimate=pl.CostEstimate(flops=STRAIGHT_FIRST, bytes_accessed=10**6, transcendentals=0),
    )(*parts)


def place_kernel(wide_ref, d_ref, y_ref, relayed_ref, out_ref, wide_s, sem):
    _, rows, clips = wide_ref.shape
    index = lax.axis_index("own")
    core = lax.rem(index, CORES)
    chip = lax.div(index, CORES)

    def put(value, flip, core_of):
        at = pl.multiple_of((lax.bitwise_xor(chip, flip) * CORES + core_of) * clips, clips)
        wide_s[:, pl.ds(at, clips)] = value.astype(F32)

    put(wide_ref[0], 0, core)
    put(wide_ref[1], 1, core)
    put(wide_ref[2], 1, 1 - core)
    put(y_ref[core], 2, core)
    put(d_ref[core], 3, core)
    put(relayed_ref[0], 3, 1 - core)
    put(relayed_ref[1], 2, 1 - core)
    put(relayed_ref[2], 0, 1 - core)
    copy = pltpu.make_async_copy(wide_s, out_ref, sem)
    copy.start()
    copy.wait()


def place(*parts):
    rows, clips = parts[0].shape[1:]
    wide = (rows, 8 * clips)
    return pl.pallas_call(
        place_kernel,
        out_shape=jax.ShapeDtypeStruct(wide, F32),
        in_specs=[VMEM] * len(parts),
        out_specs=HBM,
        scratch_shapes=[pltpu.VMEM(wide, F32), pltpu.SemaphoreType.DMA(())],
        compiler_params=pltpu.CompilerParams(vmem_limit_bytes=SMALL_VMEM),
    )(*parts)


def per_device_exchanged(planes, queries, block_ids, left_factor, right_factor, clip_grads, lengths):
    size = 4 * CORES

    def move(x, to):
        return lax.ppermute(x, "own", [(i, to(i // CORES, i % CORES)) for i in range(size)])

    def sibling(x):
        return move(x, lambda chip, core: chip * CORES + 1 - core)

    def across(x, flips):
        return move(x, lambda chip, core: (chip ^ flips[core]) * CORES + core)

    def plane(x, step):
        return lax.ppermute(x, "qry", [(i, i ^ step) for i in range(planes)])

    flips_a, flips_b = (1, 2), (2, 1)
    row, fac = pack(queries[0], block_ids, left_factor, right_factor)
    slot_d = across(row, (3, 3))
    slot_a = across(row, flips_a)
    held, again = join(fac, plane(fac, 1), row, left_factor)
    factors = [held]
    step = 2
    while step < planes:
        got = plane(held, step)
        factors.append(got)
        if step * 2 < planes:
            held = jnp.concatenate([held, got])
        step *= 2
    slot_b = across(again, flips_b)
    order_a, order_b = left_factor.shape[2], right_factor.shape[2]
    left_all, right_all = place_factors(factors, left_factor.shape[0], order_a, order_b)
    prepared = early([row, slot_d, slot_a, slot_b], left_all, right_all, order_a, order_b)
    passed = [sibling(row), sibling(slot_d), sibling(slot_a), sibling(slot_b)]
    home, near, x, cross, y, d = score(passed, prepared, left_all, right_all, clip_grads, lengths)
    y, d = across(y, (2, 2)), across(d, (3, 3))
    x, cross = across(x, (1, 1)), move(cross, lambda chip, core: (chip ^ 1) * CORES + 1 - core)
    return place(widen(home, x, cross), d, y, sibling(relay(d, y, near)))[None]


def solution(mesh):
    owners, planes = mesh.shape["own"], mesh.shape["qry"]

    def per_device(queries, block_ids, left_factor, right_factor, clip_grads, lengths):
        whole_tiles = left_factor.shape[1] % 16 == 0 and right_factor.shape[1] % 16 == 0
        whole_tiles = whole_tiles and left_factor.shape[0] * left_factor.shape[2] == LANES == right_factor.shape[2]
        if owners == 4 * CORES and planes > 1 and planes & (planes - 1) == 0 and whole_tiles:
            return per_device_exchanged(
                planes, queries, block_ids, left_factor, right_factor, clip_grads, lengths
            )
        return per_device_gathered(queries, block_ids, left_factor, right_factor, clip_grads, lengths)

    in_specs = (
        P("qry", "own", None),
        P("qry", "own"),
        P(None, "qry", None),
        P(None, "qry", None),
        P("own", None),
        P("own"),
    )
    out_specs = P("qry", "own", None)
    return jax.shard_map(
        per_device, mesh=mesh, in_specs=in_specs, out_specs=out_specs, check_vma=False
    )
```

```python
import jax
import jax.numpy as jnp
from jax import lax
from jax.experimental import pallas as pl
from jax.experimental.pallas import tpu as pltpu
from jax.sharding import PartitionSpec as P

LANES = 128
CORES = 2
SOME_VMEM = 16 << 20
SMALL_VMEM = 8 << 20
FACTORS_FIRST = 6 * 10**9
STRAIGHT_FIRST = 10**10
VMEM = pl.BlockSpec(memory_space=pltpu.VMEM)
HBM = pl.BlockSpec(memory_space=pltpu.HBM)
F32 = jnp.float32
BF16 = jnp.bfloat16


def precondition(rows, id_values, left_full, right_full):
    blocks = left_full.shape[0]
    order_a = left_full.shape[1]
    order_b = right_full.shape[1]
    labels = jnp.arange(blocks)
    onehot = (id_values[:, :, None] == labels[None, None, :]).astype(F32)
    left_rows = jnp.einsum("srk,kac->srac", onehot, left_full.astype(F32), precision=lax.Precision.HIGHEST)
    right_rows = jnp.einsum("srk,kde->srde", onehot, right_full.astype(F32), precision=lax.Precision.HIGHEST)
    matrix = rows.reshape(rows.shape[0], rows.shape[1], order_a, order_b).astype(F32)
    inner = jnp.einsum("srac,srcd->srad", left_rows, matrix, precision=lax.Precision.HIGHEST)
    outer = jnp.einsum("srad,srde->srae", inner, right_rows, precision=lax.Precision.HIGHEST)
    return outer.reshape(rows.shape).astype(BF16)


def per_device_gathered(queries, block_ids, left_factor, right_factor, clip_grads, lengths):
    left_full = lax.all_gather(left_factor, "qry", axis=1, tiled=True)
    right_full = lax.all_gather(right_factor, "qry", axis=1, tiled=True)
    prepared = precondition(queries, block_ids, left_full, right_full)
    tiles = jnp.einsum(
        "srw,cw->src",
        lax.all_gather(prepared, "own", axis=1, tiled=True),
        clip_grads,
        preferred_element_type=F32,
    )
    factor = lax.rsqrt(F32(queries.shape[2]) * lengths.astype(F32))
    return lax.all_to_all(tiles * factor[None, None, :], "own", split_axis=1, concat_axis=2, tiled=True)


def pack_kernel(q_hbm, ids_hbm, left_hbm, right_hbm, row_ref, fac_ref, ids_s, left_s, sems):
    rows, width = q_hbm.shape
    blocks, cut, order_a = left_s.shape
    copies = [
        pltpu.make_async_copy(ids_hbm, ids_s, sems.at[1]),
        pltpu.make_async_copy(left_hbm, left_s, sems.at[2]),
        pltpu.make_async_copy(right_hbm, fac_ref.at[0, :, cut:, :], sems.at[3]),
    ]
    part = width // 4
    copies = [
        pltpu.make_async_copy(
            q_hbm.at[:, i * part : (i + 1) * part], row_ref.at[:, i * part : (i + 1) * part], sems.at[4 + i]
        )
        for i in range(4)
    ] + copies
    for copy in copies:
        copy.start()
    fac_ref[0, :, :cut, order_a:] = jnp.zeros((blocks, cut, LANES - order_a), BF16)
    square = (rows, rows)
    diagonal = lax.broadcasted_iota(jnp.int32, square, 0) == lax.broadcasted_iota(jnp.int32, square, 1)
    copies[4].wait()
    labels = jnp.where(diagonal, jnp.broadcast_to(ids_s[...].astype(F32), square), 0.0)
    column = jnp.sum(labels, axis=1, keepdims=True)
    column = jnp.broadcast_to(column, (rows, LANES)).astype(BF16)
    row_ref[:, width:] = column
    copies[5].wait()
    fac_ref[0, :, :cut, :order_a] = left_s[...]
    for copy in copies[:4] + copies[6:]:
        copy.wait()


def in_hbm(x):
    return pltpu.with_memory_space_constraint(x, pltpu.HBM)


def pack(queries, block_ids, left, right):
    rows, width = queries.shape
    blocks, cut = left.shape[:2]
    depth = cut + right.shape[1]
    return pl.pallas_call(
        pack_kernel,
        out_shape=(
            jax.ShapeDtypeStruct((rows, width + LANES), BF16),
            jax.ShapeDtypeStruct((1, blocks, depth, LANES), BF16),
        ),
        in_specs=[HBM] * 4,
        out_specs=(VMEM, VMEM),
        scratch_shapes=[
            pltpu.VMEM(block_ids.shape, block_ids.dtype),
            pltpu.VMEM(left.shape, left.dtype),
            pltpu.SemaphoreType.DMA((8,)),
        ],
        compiler_params=pltpu.CompilerParams(vmem_limit_bytes=SOME_VMEM),
    )(*(in_hbm(x) for x in (queries, block_ids, left, right)))


def prepare(slots, left_all, right_all, in_s, mid_s, out_s, prep_ref):
    rows = slots[0].shape[0]
    order_a = left_all.shape[1]
    blocks = left_all.shape[0] // order_a
    order_b = right_all.shape[1] // blocks
    width = order_a * order_b
    pair = 2 * rows

    def label_of(group, n):
        row = slots[2 * group + n // rows][n % rows : n % rows + 1, width:]
        return row.astype(F32)

    for group in range(len(slots) // 2):
        both = slots[2 * group : 2 * group + 2]
        tiles = [
            jnp.concatenate([ref[:, a * order_b : (a + 1) * order_b] for ref in both], axis=0) for a in range(order_a)
        ]
        in_s[group] = jnp.swapaxes(jnp.stack(tiles), 0, 1)
    for group in range(len(slots) // 2):
        for n in range(0, pair, 2):
            x = jnp.concatenate([in_s[group, n + j] for j in range(2)], axis=1)
            inner = jnp.dot(left_all, x, preferred_element_type=F32)
            for j in range(2):
                label = label_of(group, n + j)
                one = inner[:order_a, j * order_b : (j + 1) * order_b]
                for k in range(1, blocks):
                    one = jnp.where(
                        label > k - 0.5,
                        inner[k * order_a : (k + 1) * order_a, j * order_b : (j + 1) * order_b],
                        one,
                    )
                high = one.astype(BF16)
                mid_s[group, n + j, :, :order_b] = high
                mid_s[group, n + j, :, order_b:] = (one - high.astype(F32)).astype(BF16)
    for group in range(len(slots) // 2):
        middle = mid_s[group].reshape(pair * order_a, 2 * order_b)
        outer = jnp.dot(middle, right_all, preferred_element_type=F32)
        for n in range(pair):
            label = label_of(group, n)
            one = outer[n * order_a : (n + 1) * order_a, :order_b]
            for k in range(1, blocks):
                one = jnp.where(
                    label > k - 0.5, outer[n * order_a : (n + 1) * order_a, k * order_b : (k + 1) * order_b], one
                )
            out_s[group, n] = one.astype(BF16)
    for group in range(len(slots) // 2):
        turned = jnp.swapaxes(out_s[group], 0, 1)
        for a in range(order_a):
            prep_ref[group * pair : (group + 1) * pair, a * order_b : (a + 1) * order_b] = turned[a]


def factor_kernel(order_a, order_b, *refs):
    left_ref, right_ref = refs[-2:]
    pieces = [(ref, i) for ref in refs[:-2] for i in range(ref.shape[0])]
    blocks = right_ref.shape[1] // order_b
    cut_a, cut_b = order_a // len(pieces), order_b // len(pieces)
    plane = lax.axis_index("qry")
    for m, (ref, i) in enumerate(pieces):
        piece = ref[i]
        at = lax.bitwise_xor(plane, m)
        for k in range(blocks):
            left_ref[pl.ds(pl.multiple_of(k * order_a + at * cut_a, 16), cut_a), :] = piece[
                :cut_a, k * order_a : (k + 1) * order_a
            ]
            for half in range(2):
                right_ref[
                    pl.ds(pl.multiple_of(half * order_b + at * cut_b, 16), cut_b),
                    k * order_b : (k + 1) * order_b,
                ] = piece[cut_a + k * cut_b : cut_a + (k + 1) * cut_b, :]


def place_factors(factors, blocks, order_a, order_b):
    return pl.pallas_call(
        lambda *refs: factor_kernel(order_a, order_b, *refs),
        out_shape=(
            jax.ShapeDtypeStruct((blocks * order_a, order_a), BF16),
            jax.ShapeDtypeStruct((2 * order_b, blocks * order_b), BF16),
        ),
        in_specs=[VMEM] * len(factors),
        out_specs=(VMEM, VMEM),
        compiler_params=pltpu.CompilerParams(vmem_limit_bytes=SMALL_VMEM),
        cost_estimate=pl.CostEstimate(flops=FACTORS_FIRST, bytes_accessed=10**6, transcendentals=0),
    )(*factors)


def early_kernel(nslots, *refs):
    slots = refs[:nslots]
    left_ref, right_ref, prep_ref, in_s, mid_s, out_s = refs[nslots:]
    prepare(slots, left_ref[...], right_ref[...], in_s, mid_s, out_s, prep_ref)


def early(slots, left_all, right_all, order_a, order_b):
    rows = slots[0].shape[0]
    total = len(slots) * rows
    width = order_a * order_b
    return pl.pallas_call(
        lambda *refs: early_kernel(len(slots), *refs),
        out_shape=jax.ShapeDtypeStruct((total, width), BF16),
        in_specs=[VMEM] * (len(slots) + 2),
        out_specs=VMEM,
        scratch_shapes=[
            pltpu.VMEM((len(slots) // 2, 2 * rows, order_a, wide * order_b), BF16) for wide in (1, 2, 1)
        ],
        compiler_params=pltpu.CompilerParams(vmem_limit_bytes=SOME_VMEM),
        cost_estimate=pl.CostEstimate(flops=8 * total * width * order_b, bytes_accessed=4 * total * width, transcendentals=0),
    )(*slots, left_all, right_all)


def score_kernel(nslots, *refs):
    slots = refs[:nslots]
    early_ref, left_ref, right_ref, clips_ref, len_ref = refs[nslots : nslots + 5]
    home_ref, near_ref, x_ref, cross_ref, y_ref, d_ref, in_s, mid_s, out_s, prep_s, all_s = refs[nslots + 5 :]
    width = clips_ref.shape[1]
    rows = slots[0].shape[0]
    prepare(slots, left_ref[...], right_ref[...], in_s, mid_s, out_s, prep_s)

    @pl.when(lax.axis_index("qry") >= 0)
    def _():
        queries = jnp.concatenate([early_ref[...], prep_s[...]], axis=0)
        raw = lax.dot_general(clips_ref[...], queries, (((1,), (1,)), ((), ())), preferred_element_type=F32)
        factor = lax.rsqrt(F32(width) * len_ref[...].astype(F32))
        scores = raw.T * factor
        core = lax.rem(lax.axis_index("own"), CORES)
        for j, (mine, other) in enumerate(((0, 0), (3, 3), (1 + core, 2 - core), (2 - core, 1 + core))):
            at = j * rows
            all_s[mine, core] = scores[at : at + rows].astype(BF16)
            at += scores.shape[0] // 2
            all_s[other, 1 - core] = scores[at : at + rows].astype(BF16)
        home_ref[...] = scores[:rows]
        near_ref[...] = all_s[0, 1 - core]
        x_ref[...] = all_s[1, core]
        cross_ref[...] = all_s[1, 1 - core]
        y_ref[...] = all_s[2]
        d_ref[...] = all_s[3]


def score(slots, prepared, left_all, right_all, clip_grads, lengths):
    rows = slots[0].shape[0]
    clips, width = clip_grads.shape
    order_a = left_all.shape[1]
    total = prepared.shape[0] + len(slots) * rows
    return pl.pallas_call(
        lambda *refs: score_kernel(len(slots), *refs),
        out_shape=(
            jax.ShapeDtypeStruct((rows, clips), F32),
            *(jax.ShapeDtypeStruct((rows, clips), BF16),) * 3,
            *(jax.ShapeDtypeStruct((2, rows, clips), BF16),) * 2,
        ),
        in_specs=[VMEM] * (len(slots) + 5),
        out_specs=(VMEM,) * 6,
        scratch_shapes=[
            pltpu.VMEM((len(slots) // 2, 2 * rows, order_a, wide * width // order_a), BF16) for wide in (1, 2, 1)
        ]
        + [pltpu.VMEM((len(slots) * rows, width), BF16), pltpu.VMEM((4, 2, rows, clips), BF16)],
        compiler_params=pltpu.CompilerParams(vmem_limit_bytes=SOME_VMEM),
        cost_estimate=pl.CostEstimate(
            flops=2 * total * width * (clips + 1000), bytes_accessed=clips * width * 2, transcendentals=0
        ),
    )(*slots, prepared, left_all, right_all, clip_grads, lengths.reshape(1, clips))


def join_kernel(order_a, cut, first_ref, second_ref, row_ref, both_ref, again_ref):
    blocks, depth = first_ref.shape[1:3]
    for j, ref in enumerate((first_ref, second_ref)):
        for k in range(blocks):
            both_ref[j, :cut, k * order_a : (k + 1) * order_a] = ref[0, k, :cut, :order_a]
            at = cut + k * (depth - cut)
            both_ref[j, at : at + depth - cut, :] = ref[0, k, cut:, :]
    again_ref[...] = row_ref[...]


def join(first, second, row, left):
    blocks, cut, order_a = left.shape
    rows = cut + blocks * (first.shape[2] - cut)
    return pl.pallas_call(
        lambda *refs: join_kernel(order_a, cut, *refs),
        out_shape=(
            jax.ShapeDtypeStruct((2, rows, LANES), first.dtype),
            jax.ShapeDtypeStruct(row.shape, row.dtype),
        ),
        in_specs=[VMEM] * 3,
        out_specs=(VMEM, VMEM),
        compiler_params=pltpu.CompilerParams(vmem_limit_bytes=SMALL_VMEM),
    )(first, second, row)


def relay_kernel(d_ref, y_ref, near_ref, out_ref):
    other = 1 - lax.rem(lax.axis_index("own"), CORES)
    out_ref[0] = d_ref[other]
    out_ref[1] = y_ref[other]
    out_ref[2] = near_ref[...]


def relay(d, y, near):
    return pl.pallas_call(
        relay_kernel,
        out_shape=jax.ShapeDtypeStruct((3,) + near.shape, near.dtype),
        in_specs=[VMEM] * 3,
        out_specs=VMEM,
        compiler_params=pltpu.CompilerParams(vmem_limit_bytes=SMALL_VMEM),
    )(d, y, near)


def widen_kernel(home_ref, x_ref, cross_ref, out_ref):
    for j, ref in enumerate((home_ref, x_ref, cross_ref)):
        out_ref[j] = ref[...].astype(F32)


def widen(*parts):
    return pl.pallas_call(
        widen_kernel,
        out_shape=jax.ShapeDtypeStruct((len(parts),) + parts[0].shape, F32),
        in_specs=[VMEM] * len(parts),
        out_specs=VMEM,
        compiler_params=pltpu.CompilerParams(vmem_limit_bytes=SMALL_VMEM),
        cost_estimate=pl.CostEstimate(flops=STRAIGHT_FIRST, bytes_accessed=10**6, transcendentals=0),
    )(*parts)


def place_kernel(wide_ref, d_ref, y_ref, relayed_ref, out_ref, wide_s, sems):
    _, rows, clips = wide_ref.shape
    index = lax.axis_index("own")
    core = lax.rem(index, CORES)
    chip = lax.div(index, CORES)

    copies = []

    def put(value, flip, core_of):
        at = pl.ds(pl.multiple_of((lax.bitwise_xor(chip, flip) * CORES + core_of) * clips, clips), clips)
        wide_s[:, at] = value.astype(F32)
        copies.append(pltpu.make_async_copy(wide_s.at[:, at], out_ref.at[:, at], sems.at[len(copies)]))
        copies[-1].start()

    put(relayed_ref[0], 3, 1 - core)
    put(relayed_ref[1], 2, 1 - core)
    put(relayed_ref[2], 0, 1 - core)
    put(y_ref[core], 2, core)
    put(d_ref[core], 3, core)
    put(wide_ref[0], 0, core)
    put(wide_ref[1], 1, core)
    put(wide_ref[2], 1, 1 - core)
    for copy in copies:
        copy.wait()


def place(*parts):
    rows, clips = parts[0].shape[1:]
    wide = (rows, 8 * clips)
    return pl.pallas_call(
        place_kernel,
        out_shape=jax.ShapeDtypeStruct(wide, F32),
        in_specs=[VMEM] * len(parts),
        out_specs=HBM,
        scratch_shapes=[pltpu.VMEM(wide, F32), pltpu.SemaphoreType.DMA((8,))],
        compiler_params=pltpu.CompilerParams(vmem_limit_bytes=SMALL_VMEM),
    )(*parts)


def per_device_exchanged(planes, queries, block_ids, left_factor, right_factor, clip_grads, lengths):
    size = 4 * CORES

    def move(x, to):
        return lax.ppermute(x, "own", [(i, to(i // CORES, i % CORES)) for i in range(size)])

    def sibling(x):
        return move(x, lambda chip, core: chip * CORES + 1 - core)

    def across(x, flips):
        return move(x, lambda chip, core: (chip ^ flips[core]) * CORES + core)

    def plane(x, step):
        return lax.ppermute(x, "qry", [(i, i ^ step) for i in range(planes)])

    flips_a, flips_b = (1, 2), (2, 1)
    row, fac = pack(queries[0], block_ids, left_factor, right_factor)
    slot_d = across(row, (3, 3))
    slot_a = across(row, flips_a)
    held, again = join(fac, plane(fac, 1), row, left_factor)
    factors = [held]
    step = 2
    while step < planes:
        got = plane(held, step)
        factors.append(got)
        if step * 2 < planes:
            held = jnp.concatenate([held, got])
        step *= 2
    slot_b = across(again, flips_b)
    order_a, order_b = left_factor.shape[2], right_factor.shape[2]
    left_all, right_all = place_factors(factors, left_factor.shape[0], order_a, order_b)
    prepared = early([row, slot_d, slot_a, slot_b], left_all, right_all, order_a, order_b)
    passed = [sibling(row), sibling(slot_d), sibling(slot_a), sibling(slot_b)]
    home, near, x, cross, y, d = score(passed, prepared, left_all, right_all, clip_grads, lengths)
    y, d = across(y, (2, 2)), across(d, (3, 3))
    x, cross = across(x, (1, 1)), move(cross, lambda chip, core: (chip ^ 1) * CORES + 1 - core)
    return place(widen(home, x, cross), d, y, sibling(relay(d, y, near)))[None]


def solution(mesh):
    owners, planes = mesh.shape["own"], mesh.shape["qry"]

    def per_device(queries, block_ids, left_factor, right_factor, clip_grads, lengths):
        whole_tiles = left_factor.shape[1] % 16 == 0 and right_factor.shape[1] % 16 == 0
        whole_tiles = whole_tiles and left_factor.shape[0] * left_factor.shape[2] == LANES == right_factor.shape[2]
        if owners == 4 * CORES and planes > 1 and planes & (planes - 1) == 0 and whole_tiles:
            return per_device_exchanged(
                planes, queries, block_ids, left_factor, right_factor, clip_grads, lengths
            )
        return per_device_gathered(queries, block_ids, left_factor, right_factor, clip_grads, lengths)

    in_specs = (
        P("qry", "own", None),
        P("qry", "own"),
        P(None, "qry", None),
        P(None, "qry", None),
        P("own", None),
        P("own"),
    )
    out_specs = P("qry", "own", None)
    return jax.shard_map(
        per_device, mesh=mesh, in_specs=in_specs, out_specs=out_specs, check_vma=False
    )
```

```python
import jax
import jax.numpy as jnp
from jax import lax
from jax.experimental import pallas as pl
from jax.experimental.pallas import tpu as pltpu
from jax.sharding import PartitionSpec as P

LANES = 128
CORES = 2
SOME_VMEM = 16 << 20
SMALL_VMEM = 8 << 20
FACTORS_FIRST = 6 * 10**9
STRAIGHT_FIRST = 10**10
VMEM = pl.BlockSpec(memory_space=pltpu.VMEM)
HBM = pl.BlockSpec(memory_space=pltpu.HBM)
F32 = jnp.float32
BF16 = jnp.bfloat16


def precondition(rows, id_values, left_full, right_full):
    blocks = left_full.shape[0]
    order_a = left_full.shape[1]
    order_b = right_full.shape[1]
    labels = jnp.arange(blocks)
    onehot = (id_values[:, :, None] == labels[None, None, :]).astype(F32)
    left_rows = jnp.einsum("srk,kac->srac", onehot, left_full.astype(F32), precision=lax.Precision.HIGHEST)
    right_rows = jnp.einsum("srk,kde->srde", onehot, right_full.astype(F32), precision=lax.Precision.HIGHEST)
    matrix = rows.reshape(rows.shape[0], rows.shape[1], order_a, order_b).astype(F32)
    inner = jnp.einsum("srac,srcd->srad", left_rows, matrix, precision=lax.Precision.HIGHEST)
    outer = jnp.einsum("srad,srde->srae", inner, right_rows, precision=lax.Precision.HIGHEST)
    return outer.reshape(rows.shape).astype(BF16)


def per_device_gathered(queries, block_ids, left_factor, right_factor, clip_grads, lengths):
    left_full = lax.all_gather(left_factor, "qry", axis=1, tiled=True)
    right_full = lax.all_gather(right_factor, "qry", axis=1, tiled=True)
    prepared = precondition(queries, block_ids, left_full, right_full)
    tiles = jnp.einsum(
        "srw,cw->src",
        lax.all_gather(prepared, "own", axis=1, tiled=True),
        clip_grads,
        preferred_element_type=F32,
    )
    factor = lax.rsqrt(F32(queries.shape[2]) * lengths.astype(F32))
    return lax.all_to_all(tiles * factor[None, None, :], "own", split_axis=1, concat_axis=2, tiled=True)


def pack_kernel(q_hbm, ids_hbm, left_hbm, right_hbm, row_ref, fac_ref, ids_s, left_s, sems):
    rows, width = q_hbm.shape
    blocks, cut, order_a = left_s.shape
    copies = [
        pltpu.make_async_copy(ids_hbm, ids_s, sems.at[1]),
        pltpu.make_async_copy(left_hbm, left_s, sems.at[2]),
        pltpu.make_async_copy(right_hbm, fac_ref.at[0, :, cut:, :], sems.at[3]),
    ]
    part = width // 4
    copies = [
        pltpu.make_async_copy(
            q_hbm.at[:, i * part : (i + 1) * part], row_ref.at[:, i * part : (i + 1) * part], sems.at[4 + i]
        )
        for i in range(4)
    ] + copies
    for copy in copies:
        copy.start()
    fac_ref[0, :, :cut, order_a:] = jnp.zeros((blocks, cut, LANES - order_a), BF16)
    square = (rows, rows)
    diagonal = lax.broadcasted_iota(jnp.int32, square, 0) == lax.broadcasted_iota(jnp.int32, square, 1)
    copies[4].wait()
    labels = jnp.where(diagonal, jnp.broadcast_to(ids_s[...].astype(F32), square), 0.0)
    column = jnp.sum(labels, axis=1, keepdims=True)
    column = jnp.broadcast_to(column, (rows, LANES)).astype(BF16)
    row_ref[:, width:] = column
    copies[5].wait()
    fac_ref[0, :, :cut, :order_a] = left_s[...]
    for copy in copies[:4] + copies[6:]:
        copy.wait()


def in_hbm(x):
    return pltpu.with_memory_space_constraint(x, pltpu.HBM)


def pack(queries, block_ids, left, right):
    rows, width = queries.shape
    blocks, cut = left.shape[:2]
    depth = cut + right.shape[1]
    return pl.pallas_call(
        pack_kernel,
        out_shape=(
            jax.ShapeDtypeStruct((rows, width + LANES), BF16),
            jax.ShapeDtypeStruct((1, blocks, depth, LANES), BF16),
        ),
        in_specs=[HBM] * 4,
        out_specs=(VMEM, VMEM),
        scratch_shapes=[
            pltpu.VMEM(block_ids.shape, block_ids.dtype),
            pltpu.VMEM(left.shape, left.dtype),
            pltpu.SemaphoreType.DMA((8,)),
        ],
        compiler_params=pltpu.CompilerParams(vmem_limit_bytes=SOME_VMEM),
    )(*(in_hbm(x) for x in (queries, block_ids, left, right)))


def prepare(slots, left_all, right_all, in_s, mid_s, out_s, prep_ref):
    rows = slots[0].shape[0]
    order_a = left_all.shape[1]
    blocks = left_all.shape[0] // order_a
    order_b = right_all.shape[1] // blocks
    width = order_a * order_b
    pair = 2 * rows

    def label_of(group, n):
        row = slots[2 * group + n // rows][n % rows : n % rows + 1, width:]
        return row.astype(F32)

    for group in range(len(slots) // 2):
        both = slots[2 * group : 2 * group + 2]
        tiles = [
            jnp.concatenate([ref[:, a * order_b : (a + 1) * order_b] for ref in both], axis=0) for a in range(order_a)
        ]
        in_s[group] = jnp.swapaxes(jnp.stack(tiles), 0, 1)
    for group in range(len(slots) // 2):
        for n in range(0, pair, 2):
            x = jnp.concatenate([in_s[group, n + j] for j in range(2)], axis=1)
            inner = jnp.dot(left_all, x, preferred_element_type=F32)
            for j in range(2):
                label = label_of(group, n + j)
                one = inner[:order_a, j * order_b : (j + 1) * order_b]
                for k in range(1, blocks):
                    one = jnp.where(
                        label > k - 0.5,
                        inner[k * order_a : (k + 1) * order_a, j * order_b : (j + 1) * order_b],
                        one,
                    )
                high = one.astype(BF16)
                mid_s[group, n + j, :, :order_b] = high
                mid_s[group, n + j, :, order_b:] = (one - high.astype(F32)).astype(BF16)
    for group in range(len(slots) // 2):
        middle = mid_s[group].reshape(pair * order_a, 2 * order_b)
        outer = jnp.dot(middle, right_all, preferred_element_type=F32)
        for n in range(pair):
            label = label_of(group, n)
            one = outer[n * order_a : (n + 1) * order_a, :order_b]
            for k in range(1, blocks):
                one = jnp.where(
                    label > k - 0.5, outer[n * order_a : (n + 1) * order_a, k * order_b : (k + 1) * order_b], one
                )
            out_s[group, n] = one.astype(BF16)
    for group in range(len(slots) // 2):
        turned = jnp.swapaxes(out_s[group], 0, 1)
        for a in range(order_a):
            prep_ref[group * pair : (group + 1) * pair, a * order_b : (a + 1) * order_b] = turned[a]


def factor_kernel(order_a, order_b, *refs):
    left_ref, right_ref = refs[-2:]
    pieces = [(ref, i) for ref in refs[:-2] for i in range(ref.shape[0])]
    blocks = right_ref.shape[1] // order_b
    cut_a, cut_b = order_a // len(pieces), order_b // len(pieces)
    plane = lax.axis_index("qry")
    for m, (ref, i) in enumerate(pieces):
        piece = ref[i]
        at = lax.bitwise_xor(plane, m)
        for k in range(blocks):
            left_ref[pl.ds(pl.multiple_of(k * order_a + at * cut_a, 16), cut_a), :] = piece[
                :cut_a, k * order_a : (k + 1) * order_a
            ]
            for half in range(2):
                right_ref[
                    pl.ds(pl.multiple_of(half * order_b + at * cut_b, 16), cut_b),
                    k * order_b : (k + 1) * order_b,
                ] = piece[cut_a + k * cut_b : cut_a + (k + 1) * cut_b, :]


def place_factors(factors, blocks, order_a, order_b):
    return pl.pallas_call(
        lambda *refs: factor_kernel(order_a, order_b, *refs),
        out_shape=(
            jax.ShapeDtypeStruct((blocks * order_a, order_a), BF16),
            jax.ShapeDtypeStruct((2 * order_b, blocks * order_b), BF16),
        ),
        in_specs=[VMEM] * len(factors),
        out_specs=(VMEM, VMEM),
        compiler_params=pltpu.CompilerParams(vmem_limit_bytes=SMALL_VMEM),
        cost_estimate=pl.CostEstimate(flops=FACTORS_FIRST, bytes_accessed=10**6, transcendentals=0),
    )(*factors)


def early_kernel(nslots, *refs):
    slots = refs[:nslots]
    left_ref, right_ref, prep_ref, in_s, mid_s, out_s = refs[nslots:]
    prepare(slots, left_ref[...], right_ref[...], in_s, mid_s, out_s, prep_ref)


def early(slots, left_all, right_all, order_a, order_b):
    rows = slots[0].shape[0]
    total = len(slots) * rows
    width = order_a * order_b
    return pl.pallas_call(
        lambda *refs: early_kernel(len(slots), *refs),
        out_shape=jax.ShapeDtypeStruct((total, width), BF16),
        in_specs=[VMEM] * (len(slots) + 2),
        out_specs=VMEM,
        scratch_shapes=[
            pltpu.VMEM((len(slots) // 2, 2 * rows, order_a, wide * order_b), BF16) for wide in (1, 2, 1)
        ],
        compiler_params=pltpu.CompilerParams(vmem_limit_bytes=SOME_VMEM),
        cost_estimate=pl.CostEstimate(flops=8 * total * width * order_b, bytes_accessed=4 * total * width, transcendentals=0),
    )(*slots, left_all, right_all)


def score_kernel(nslots, *refs):
    slots = refs[:nslots]
    early_ref, left_ref, right_ref, clips_ref, len_ref = refs[nslots : nslots + 5]
    home_ref, near_ref, x_ref, cross_ref, y_ref, d_ref, in_s, mid_s, out_s, prep_s = refs[nslots + 5 :]
    width = clips_ref.shape[1]
    rows = slots[0].shape[0]
    prepare(slots, left_ref[...], right_ref[...], in_s, mid_s, out_s, prep_s)

    @pl.when(lax.axis_index("qry") >= 0)
    def _():
        queries = jnp.concatenate([early_ref[...], prep_s[...]], axis=0)
        raw = lax.dot_general(clips_ref[...], queries, (((1,), (1,)), ((), ())), preferred_element_type=F32)
        factor = lax.rsqrt(F32(width) * len_ref[...].astype(F32))
        scores = raw.T * factor
        core = lax.rem(lax.axis_index("own"), CORES)
        home_ref[...] = scores[:rows]

        def send(own):
            block = {}
            for j, (mine, other) in enumerate(((0, 0), (3, 3), (1 + own, 2 - own), (2 - own, 1 + own))):
                at = j * rows
                block[mine, own] = scores[at : at + rows].astype(BF16)
                at += scores.shape[0] // 2
                block[other, 1 - own] = scores[at : at + rows].astype(BF16)
            near_ref[...] = block[0, 1 - own]
            x_ref[...] = block[1, own]
            cross_ref[...] = block[1, 1 - own]
            for of in range(CORES):
                y_ref[of] = block[2, of]
                d_ref[of] = block[3, of]

        for own in range(CORES):
            pl.when(core == own)(lambda own=own: send(own))


def score(slots, prepared, left_all, right_all, clip_grads, lengths):
    rows = slots[0].shape[0]
    clips, width = clip_grads.shape
    order_a = left_all.shape[1]
    total = prepared.shape[0] + len(slots) * rows
    return pl.pallas_call(
        lambda *refs: score_kernel(len(slots), *refs),
        out_shape=(
            jax.ShapeDtypeStruct((rows, clips), F32),
            *(jax.ShapeDtypeStruct((rows, clips), BF16),) * 3,
            *(jax.ShapeDtypeStruct((2, rows, clips), BF16),) * 2,
        ),
        in_specs=[VMEM] * (len(slots) + 5),
        out_specs=(VMEM,) * 6,
        scratch_shapes=[
            pltpu.VMEM((len(slots) // 2, 2 * rows, order_a, wide * width // order_a), BF16) for wide in (1, 2, 1)
        ]
        + [pltpu.VMEM((len(slots) * rows, width), BF16)],
        compiler_params=pltpu.CompilerParams(vmem_limit_bytes=SOME_VMEM),
        cost_estimate=pl.CostEstimate(
            flops=2 * total * width * (clips + 1000), bytes_accessed=clips * width * 2, transcendentals=0
        ),
    )(*slots, prepared, left_all, right_all, clip_grads, lengths.reshape(1, clips))


def join_kernel(order_a, cut, first_ref, second_ref, row_ref, both_ref, again_ref):
    blocks, depth = first_ref.shape[1:3]
    for j, ref in enumerate((first_ref, second_ref)):
        for k in range(blocks):
            both_ref[j, :cut, k * order_a : (k + 1) * order_a] = ref[0, k, :cut, :order_a]
            at = cut + k * (depth - cut)
            both_ref[j, at : at + depth - cut, :] = ref[0, k, cut:, :]
    again_ref[...] = row_ref[...]


def join(first, second, row, left):
    blocks, cut, order_a = left.shape
    rows = cut + blocks * (first.shape[2] - cut)
    return pl.pallas_call(
        lambda *refs: join_kernel(order_a, cut, *refs),
        out_shape=(
            jax.ShapeDtypeStruct((2, rows, LANES), first.dtype),
            jax.ShapeDtypeStruct(row.shape, row.dtype),
        ),
        in_specs=[VMEM] * 3,
        out_specs=(VMEM, VMEM),
        compiler_params=pltpu.CompilerParams(vmem_limit_bytes=SMALL_VMEM),
    )(first, second, row)


def relay_kernel(d_ref, y_ref, near_ref, out_ref):
    other = 1 - lax.rem(lax.axis_index("own"), CORES)
    out_ref[0] = d_ref[other]
    out_ref[1] = y_ref[other]
    out_ref[2] = near_ref[...]


def relay(d, y, near):
    return pl.pallas_call(
        relay_kernel,
        out_shape=jax.ShapeDtypeStruct((3,) + near.shape, near.dtype),
        in_specs=[VMEM] * 3,
        out_specs=VMEM,
        compiler_params=pltpu.CompilerParams(vmem_limit_bytes=SMALL_VMEM),
    )(d, y, near)


def widen_kernel(home_ref, x_ref, cross_ref, out_ref):
    for j, ref in enumerate((home_ref, x_ref, cross_ref)):
        out_ref[j] = ref[...].astype(F32)


def widen(*parts):
    return pl.pallas_call(
        widen_kernel,
        out_shape=jax.ShapeDtypeStruct((len(parts),) + parts[0].shape, F32),
        in_specs=[VMEM] * len(parts),
        out_specs=VMEM,
        compiler_params=pltpu.CompilerParams(vmem_limit_bytes=SMALL_VMEM),
        cost_estimate=pl.CostEstimate(flops=STRAIGHT_FIRST, bytes_accessed=10**6, transcendentals=0),
    )(*parts)


def place_kernel(wide_ref, d_ref, y_ref, relayed_ref, out_ref, wide_s, sem):
    _, rows, clips = wide_ref.shape
    index = lax.axis_index("own")
    core = lax.rem(index, CORES)
    chip = lax.div(index, CORES)

    def put(value, flip, core_of):
        at = pl.multiple_of((lax.bitwise_xor(chip, flip) * CORES + core_of) * clips, clips)
        wide_s[:, pl.ds(at, clips)] = value.astype(F32)

    put(wide_ref[0], 0, core)
    put(wide_ref[1], 1, core)
    put(wide_ref[2], 1, 1 - core)
    put(y_ref[core], 2, core)
    put(d_ref[core], 3, core)
    put(relayed_ref[0], 3, 1 - core)
    put(relayed_ref[1], 2, 1 - core)
    put(relayed_ref[2], 0, 1 - core)
    copy = pltpu.make_async_copy(wide_s, out_ref, sem)
    copy.start()
    copy.wait()


def place(*parts):
    rows, clips = parts[0].shape[1:]
    wide = (rows, 8 * clips)
    return pl.pallas_call(
        place_kernel,
        out_shape=jax.ShapeDtypeStruct(wide, F32),
        in_specs=[VMEM] * len(parts),
        out_specs=HBM,
        scratch_shapes=[pltpu.VMEM(wide, F32), pltpu.SemaphoreType.DMA(())],
        compiler_params=pltpu.CompilerParams(vmem_limit_bytes=SMALL_VMEM),
    )(*parts)


def per_device_exchanged(planes, queries, block_ids, left_factor, right_factor, clip_grads, lengths):
    size = 4 * CORES

    def move(x, to):
        return lax.ppermute(x, "own", [(i, to(i // CORES, i % CORES)) for i in range(size)])

    def sibling(x):
        return move(x, lambda chip, core: chip * CORES + 1 - core)

    def across(x, flips):
        return move(x, lambda chip, core: (chip ^ flips[core]) * CORES + core)

    def plane(x, step):
        return lax.ppermute(x, "qry", [(i, i ^ step) for i in range(planes)])

    flips_a, flips_b = (1, 2), (2, 1)
    row, fac = pack(queries[0], block_ids, left_factor, right_factor)
    slot_d = across(row, (3, 3))
    slot_a = across(row, flips_a)
    held, again = join(fac, plane(fac, 1), row, left_factor)
    factors = [held]
    step = 2
    while step < planes:
        got = plane(held, step)
        factors.append(got)
        if step * 2 < planes:
            held = jnp.concatenate([held, got])
        step *= 2
    slot_b = across(again, flips_b)
    order_a, order_b = left_factor.shape[2], right_factor.shape[2]
    left_all, right_all = place_factors(factors, left_factor.shape[0], order_a, order_b)
    prepared = early([row, slot_d, slot_a, slot_b], left_all, right_all, order_a, order_b)
    passed = [sibling(row), sibling(slot_d), sibling(slot_a), sibling(slot_b)]
    home, near, x, cross, y, d = score(passed, prepared, left_all, right_all, clip_grads, lengths)
    y, d = across(y, (2, 2)), across(d, (3, 3))
    x, cross = across(x, (1, 1)), move(cross, lambda chip, core: (chip ^ 1) * CORES + 1 - core)
    return place(widen(home, x, cross), d, y, sibling(relay(d, y, near)))[None]


def solution(mesh):
    owners, planes = mesh.shape["own"], mesh.shape["qry"]

    def per_device(queries, block_ids, left_factor, right_factor, clip_grads, lengths):
        whole_tiles = left_factor.shape[1] % 16 == 0 and right_factor.shape[1] % 16 == 0
        whole_tiles = whole_tiles and left_factor.shape[0] * left_factor.shape[2] == LANES == right_factor.shape[2]
        if owners == 4 * CORES and planes > 1 and planes & (planes - 1) == 0 and whole_tiles:
            return per_device_exchanged(
                planes, queries, block_ids, left_factor, right_factor, clip_grads, lengths
            )
        return per_device_gathered(queries, block_ids, left_factor, right_factor, clip_grads, lengths)

    in_specs = (
        P("qry", "own", None),
        P("qry", "own"),
        P(None, "qry", None),
        P(None, "qry", None),
        P("own", None),
        P("own"),
    )
    out_specs = P("qry", "own", None)
    return jax.shard_map(
        per_device, mesh=mesh, in_specs=in_specs, out_specs=out_specs, check_vma=False
    )
```
